128 devices in a mesh: blk: 16 (over y, z), grp: 8 (over x, core).
Axes of the slice: x: 4, y: 4, z: 4, core: 2. Of those that a mesh axis runs over, the one named last changes fastest.
Arguments:
- image_embed: bfloat16 [16384, 1280], P(('blk', 'grp')), may hold values from -0.8 to 0.8
- text_embed: bfloat16 [16384, 1280], P(('blk', 'grp')), may hold values from -0.8 to 0.8
- log_scale: float32 [1], replicated, may hold values from 4 to 4.6
- pairing: int32 [16], replicated, may hold values from 0 to 15, as said below
Outputs:
- grad_image: float32 [16384, 1280], P(('blk', 'grp'))
- grad_text: float32 [16384, 1280], P(('blk', 'grp'))
- loss: float32 [1], replicated
- grad_log_scale: float32 [1], replicated
The draws below stay inside these ranges and needn't reach their ends.
Inputs may be any that keep to these rules, and one draw needn't show every extreme that they name: pairing holds each of the 16 block numbers once: the matching caption of image row r is text row pairing[r // 1024] * 1024 + r % 1024.
All inputs are finite; a program needn't handle non-finite values.
Results may differ from the reference program's by a relative error of at most 0.015.
Values may be sent and summed in bfloat16 or wider, within the bound.
A program may use at most 64 MiB of HBM per device.

```python
import jax
import jax.numpy as jnp
from jax import lax

D = 1280
ROWS_DEV = 128
BLOCK = 1024
BATCH = 16384
N_BLK = 16
N_GRP = 8


def shared_parts(key):
    order = jax.random.permutation(jax.random.fold_in(key, 11), N_BLK).astype(jnp.int32)
    common = jax.random.normal(jax.random.fold_in(key, 12), (BATCH, D), jnp.float32)
    common = jnp.clip(common, -4.0, 4.0)
    ranks = jax.random.permutation(jax.random.fold_in(key, 13), N_BLK).astype(jnp.float32)
    ladder = 0.16 + 0.2 * (ranks - 1.0) / max(N_BLK - 2, 1)
    block_mix = jnp.where(ranks < 0.5, 0.02, ladder)
    mixing = jnp.broadcast_to(block_mix[:, None, None], (N_BLK, BLOCK, 1)).reshape(BATCH, 1)
    return (order, common, mixing)


def draw_pairing(key, part):
    order, common, mixing = shared_parts(key)
    return order


def draw_image_embed(key, part):
    order, common, mixing = shared_parts(key)
    values = common
    return jnp.clip(0.03 * values, -0.8, 0.8).astype(jnp.bfloat16)


def draw_text_embed(key, part):
    order, common, mixing = shared_parts(key)
    key = jax.random.fold_in(key, 7)
    noise_key = jax.random.fold_in(key, 0)
    noise = jnp.clip(jax.random.normal(noise_key, (BATCH, D), jnp.float32), -4.0, 4.0)
    source = mixing * common + jnp.sqrt(1.0 - mixing * mixing) * noise
    placed = jnp.zeros((N_BLK, BLOCK, D), jnp.float32).at[order].set(source.reshape(N_BLK, BLOCK, D))
    placed = placed.reshape(BATCH, D)
    values = placed
    return jnp.clip(0.03 * values, -0.8, 0.8).astype(jnp.bfloat16)


def setup_inputs(seed: int = 0) -> dict:
    key_of = jax.random.split(jax.random.key(seed), 5)
    return {
        "image_embed": draw_image_embed(jax.random.fold_in(key_of[4], 71), 0),
        "text_embed": draw_text_embed(jax.random.fold_in(key_of[4], 71), 0),
        "log_scale": jnp.clip(jax.random.uniform(key_of[2], (1,), jnp.float32, 4.0, 4.6), 4.0, 4.6),
        "pairing": draw_pairing(jax.random.fold_in(key_of[4], 71), 0),
    }


softcap = 30.0

def normalize(embed):
    wide = embed.astype(jnp.float32)
    inverse = lax.rsqrt(lax.optimization_barrier(jnp.sum(wide * wide, axis=1, keepdims=True)) + 1e-06)
    unit = wide * inverse
    return (inverse, unit, unit.astype(jnp.bfloat16))

def back_norm(inverse, unit, grad_unit):
    inner = lax.optimization_barrier(jnp.sum(unit * grad_unit, axis=1, keepdims=True))
    return inverse * (grad_unit - unit * inner)

def reference(image_embed, text_embed, log_scale, pairing):
    img_inverse, img_unit, img_norm = normalize(image_embed)
    txt_inverse, txt_unit, txt_norm = normalize(text_embed)
    scale = jnp.exp(log_scale[0])
    blocks = img_norm.reshape(N_BLK, BLOCK, D)
    bases = pairing.astype(jnp.int32) * BLOCK
    txt_sets = txt_norm.astype(jnp.float32).reshape(N_BLK, N_GRP, ROWS_DEV, D)

    def logits(block_rows, base):
        cosine = jnp.dot(block_rows, txt_norm.T, preferred_element_type=jnp.float32)
        capped = softcap * jnp.tanh(scale * cosine / softcap)
        row_ids = lax.broadcasted_iota(jnp.int32, (BLOCK, BATCH), 0)
        col_ids = lax.broadcasted_iota(jnp.int32, (BLOCK, BATCH), 1)
        partner = (col_ids == row_ids + base).astype(jnp.float32)
        return (cosine, capped, partner)

    def first(col_sum, inputs):
        block_rows, base = inputs
        cosine, capped, partner = logits(block_rows, base)
        powers = jnp.exp(capped)
        return (col_sum + lax.optimization_barrier(jnp.sum(powers, axis=0)), (jnp.log(lax.optimization_barrier(jnp.sum(powers, axis=1))), jnp.sum(capped * partner)))
    col_sum, (row_lse, positive) = lax.scan(first, jnp.zeros((BATCH,), jnp.float32), (blocks, bases))
    col_lse = jnp.log(col_sum)
    loss = (jnp.sum(row_lse) + jnp.sum(col_lse) - 2.0 * jnp.sum(positive)) / (2.0 * BATCH)

    def second(carry, inputs):
        grad_txt, slope = carry
        block_rows, base, block_lse = inputs
        cosine, capped, partner = logits(block_rows, base)
        weight = 0.5 * (jnp.exp(capped - block_lse[:, None]) + jnp.exp(capped - col_lse[None, :])) - partner
        ratio = capped / softcap
        slope_term = weight * (1.0 - ratio * ratio)
        grad_logit = (scale * slope_term).astype(jnp.bfloat16)
        logit_sets = grad_logit.astype(jnp.float32).reshape(BLOCK, N_BLK, N_GRP, ROWS_DEV)
        set_parts = jnp.einsum('rbgi,bgid->grd', logit_sets, txt_sets)
        set_rounded = lax.optimization_barrier(set_parts.astype(jnp.bfloat16))
        grad_rows = lax.optimization_barrier(jnp.sum(set_rounded.astype(jnp.float32), axis=0))
        column_part = jnp.dot(grad_logit.T, block_rows, preferred_element_type=jnp.float32)
        column_rounded = lax.optimization_barrier(column_part.astype(jnp.bfloat16))
        grad_txt = grad_txt + column_rounded.astype(jnp.float32)
        return ((grad_txt, slope + jnp.sum(slope_term * cosine)), grad_rows)
    init = (jnp.zeros((BATCH, D), jnp.float32), jnp.zeros((), jnp.float32))
    (grad_txt, slope), grad_img = lax.scan(second, init, (blocks, bases, row_lse))
    grad_img = grad_img.reshape(BATCH, D)
    grad_image = back_norm(img_inverse, img_unit, grad_img)
    grad_text = back_norm(txt_inverse, txt_unit, grad_txt)
    grad_log_scale = scale * slope / BATCH
    return (grad_image, grad_text, jnp.reshape(loss, (1,)), jnp.reshape(grad_log_scale, (1,)))
```

```python
import jax
import jax.numpy as jnp
from jax import lax
from jax.experimental import pallas as pl
from jax.experimental.pallas import tpu as pltpu
from jax.sharding import PartitionSpec as P

f32, bf16 = jnp.float32, jnp.bfloat16
MESH = pl.DeviceIdType.MESH
CAP = 30.0
ROWS, D, BATCH = 128, 1280, 16384
ARRIVAL = ((0, 0), (1, 0), (3, 0), (0, 1), (2, 0), (1, 1), (3, 1), (2, 1))
REDUCE = ((2, 1), (1, 1), (3, 1), (0, 1), (2, 0), (1, 0), (3, 0), (0, 0))
LAND_AT = (0, 32, 64, 128, 192, 256, 320, 384, 448, 480, 512, 544, 576, 640, 704, 768, 832)
LAND_ROWS = (32, 32, 64, 64, 64, 64, 64, 64, 32, 32, 32, 32, 64, 64, 64, 64, 64)
LAND = 896


def flip(bit, by):
    return bit + by - 2 * bit * by


def turn(place, by):
    return lax.rem(place + by, 4)


class Messages:
    def __init__(self, send, recv):
        self.send, self.recv, self.count, self.sent = send, recv, 0, []

    def take(self, count):
        first = self.count
        self.count += count
        return first

    def start(self, k, src, dst, device):
        copy = pltpu.make_async_remote_copy(
            src, dst, self.send.at[k], self.recv.at[k], device_id=device, device_id_type=MESH
        )
        copy.start()
        self.sent.append(copy)

    def arrived(self, k, region, device):
        pltpu.make_async_remote_copy(
            region, region, self.send.at[k], self.recv.at[k], device_id=device, device_id_type=MESH
        ).wait_recv()

    def finish(self):
        for copy in self.sent:
            copy.wait_send()


class Gather:
    def __init__(self, msgs, region, plus, minus, pair, me):
        self.m, self.region, self.me = msgs, region, me
        self.plus, self.minus, self.pair = plus, minus, pair
        self.k = msgs.take(15)

    TABLE = (
        ("plus", (0, 0, 0, 64), (3, 0, 0, 64)),
        ("plus", (0, 0, 64, 64), (3, 0, 64, 64)),
        ("plus", (3, 0, 0, 64), (2, 0, 0, 64)),
        ("plus", (0, 1, 0, 64), (3, 1, 0, 64)),
        ("plus", (3, 1, 0, 32), (2, 1, 0, 32)),
        ("minus", (0, 0, 64, 64), (1, 0, 64, 64)),
        ("minus", (0, 0, 0, 64), (1, 0, 0, 64)),
        ("minus", (1, 0, 64, 64), (2, 0, 64, 64)),
        ("minus", (0, 1, 0, 64), (1, 1, 0, 64)),
        ("minus", (1, 1, 32, 32), (2, 1, 32, 32)),
        ("pair", (0, 0, 0, 64), (0, 1, 0, 64)),
        ("pair", (0, 0, 64, 64), (0, 1, 64, 64)),
        ("pair", (1, 0, 64, 64), (1, 1, 64, 64)),
        ("pair", (3, 0, 64, 64), (3, 1, 64, 64)),
        ("pair", (2, 0, 64, 64), (2, 1, 64, 64)),
    )

    def go(self, *ks):
        for k in ks:
            way, here, _ = self.TABLE[k]
            ref = self.region(*here)
            self.m.start(self.k + k, ref, ref, getattr(self, way))

    def got(self, *ks):
        for k in ks:
            self.m.arrived(self.k + k, self.region(*self.TABLE[k][2]), self.me)


class Reduce:
    TABLE = (
        ("plus", (2, 1), 0, 32),
        ("minus", (2, 1), 32, 32),
        ("pair", (2, 1), 64, 64),
        ("pair", (1, 1), 64, 64),
        ("plus", (1, 1), 0, 64),
        ("pair", (3, 1), 64, 64),
        ("minus", (3, 1), 0, 64),
        ("pair", (0, 1), 64, 64),
        ("plus", (2, 0), 0, 32),
        ("minus", (2, 0), 32, 32),
        ("plus", (2, 0), 64, 32),
        ("minus", (2, 0), 96, 32),
        ("pair", (0, 1), 0, 64),
        ("plus", (1, 0), 0, 64),
        ("plus", (1, 0), 64, 64),
        ("minus", (3, 0), 0, 64),
        ("minus", (3, 0), 64, 64),
    )

    def __init__(self, msgs, part, land, plus, minus, pair, me):
        self.m, self.part, self.land, self.me = msgs, part, land, me
        self.plus, self.minus, self.pair = plus, minus, pair
        self.k = msgs.take(17)

    def where(self, k):
        return self.land.at[pl.ds(LAND_AT[k], LAND_ROWS[k])]

    def go(self, *ks):
        for k in ks:
            way, place, low, rows = self.TABLE[k]
            self.m.start(self.k + k, self.part(place, low, rows), self.where(k), getattr(self, way))

    def got(self, *ks):
        for k in ks:
            self.m.arrived(self.k + k, self.where(k), self.me)

    def add(self, place, low, rows, *landed):
        ref = self.part(place, low, rows)
        total = ref[...].astype(f32)
        for at in landed:
            total = total + self.land[pl.ds(at, rows)].astype(f32)
        ref[...] = total.astype(bf16)

    def step(self, place):
        if place == (2, 1):
            self.go(0, 1, 2)
        if place == (1, 1):
            self.go(3)
            self.got(0)
            self.add(place, 0, 32, LAND_AT[0])
            self.go(4)
        if place == (3, 1):
            self.go(5)
            self.got(1)
            self.add(place, 32, 32, LAND_AT[1])
            self.go(6)
        if place == (0, 1):
            self.go(7)
        if place == (2, 0):
            self.go(8, 9)
            self.got(2)
            self.add(place, 64, 64, LAND_AT[2])
            self.go(10, 11)
            self.got(4, 6)
            self.add((0, 1), 0, 64, LAND_AT[4], LAND_AT[6])
            self.go(12)
        if place == (1, 0):
            self.got(8)
            self.add(place, 0, 32, LAND_AT[8])
            self.go(13)
            self.got(3)
            self.add(place, 64, 64, LAND_AT[3])
            self.got(10)
            self.add(place, 64, 32, LAND_AT[10])
            self.go(14)
        if place == (3, 0):
            self.got(9)
            self.add(place, 32, 32, LAND_AT[9])
            self.go(15)
            self.got(5)
            self.add(place, 64, 64, LAND_AT[5])
            self.got(11)
            self.add(place, 96, 32, LAND_AT[11])
            self.go(16)

    def total(self):
        self.got(13, 15, 12, 7, 14, 16)
        halves = []
        for low, landed in ((0, (13, 15, 12)), (64, (14, 16, 7))):
            total = self.part((0, 0), low, 64)[...].astype(f32)
            for k in landed:
                total = total + self.where(k)[...].astype(f32)
            halves.append(total)
        return jnp.concatenate(halves, axis=0)


def kernel(
    ls_ref, pairing_ref, img_in, txt_in,
    gi_out, gt_out, loss_out, gls_out,
    img, txt, cosr, hr, gr, rowacc, colacc, arow, bmat, slacc, posacc,
    rows_all, cols_all, sc_all, sc_mid,
    gi, gi_sib, gt, land_i, land_t,
    send, recv,
):
    blk, grp = lax.axis_index("blk"), lax.axis_index("grp")
    x, c, y, z = grp // 2, lax.rem(grp, 2), blk // 4, lax.rem(blk, 4)
    yb = lax.rem(y, 2)
    tb = 1 - yb
    yp = y + 1 - 2 * yb
    yq = lax.rem(y + 3 + 2 * yb, 4)

    def device(x_, y_, z_, c_):
        return (y_ * 4 + z_, x_ * 2 + c_)

    me = device(x, y, z, c)
    sibling = device(x, y, z, 1 - c)
    img_peers = [
        (dx, dy, dc) for dy in range(2) for dx in range(4) for dc in range(2) if (dx, dy, dc) != (0, 0, 0)
    ]
    txt_peers = [(dz, dy) for dy in range(2) for dz in range(4) if (dz, dy) != (0, 0)]

    def img_peer(dx, dy, dc):
        return device(turn(x, dx), yp if dy else y, z, 1 - c if dc else c)

    def txt_peer(dz, dy):
        return device(x, yq if dy else y, turn(z, dz), c)

    barrier = pltpu.get_barrier_semaphore()
    for p in img_peers:
        pl.semaphore_signal(barrier, inc=1, device_id=img_peer(*p), device_id_type=MESH)
    for p in txt_peers:
        pl.semaphore_signal(barrier, inc=1, device_id=txt_peer(*p), device_id_type=MESH)

    def pair_of(dx, dy):
        return flip(yb, dy) * 4 + turn(x, dx)

    def slot_of(dz, dy):
        return flip(tb, dy) * 4 + turn(z, dz)

    def img_region(dx, dy, low, rows, other=False):
        half = 1 - c if other else c
        return img.at[pair_of(dx, dy), pl.ds(pl.multiple_of(half * ROWS + low, 32), rows)]

    def txt_region(dz, dy, low, rows):
        return txt.at[slot_of(dz, dy), pl.ds(low, rows)]

    def normalize(ref):
        wide = ref[...].astype(f32)
        inverse = lax.rsqrt(jnp.sum(wide * wide, axis=1, keepdims=True) + 1e-06)
        return inverse, wide * inverse

    img_region(0, 0, 0, ROWS)[...] = normalize(img_in)[1].astype(bf16)
    txt_region(0, 0, 0, ROWS)[...] = normalize(txt_in)[1].astype(bf16)

    msgs = Messages(send, recv)
    gat_i = Gather(msgs, img_region, img_peer(1, 0, 0), img_peer(3, 0, 0), img_peer(0, 1, 0), me)
    gat_t = Gather(msgs, txt_region, txt_peer(1, 0), txt_peer(3, 0), txt_peer(0, 1), me)
    both = (gat_i, gat_t)
    sib_k = msgs.take(8)

    def share(*places):
        for place in places:
            ref = img_region(*place, 0, ROWS)
            msgs.start(sib_k + ARRIVAL.index(place), ref, ref, sibling)

    def shared(*places):
        for place in places:
            msgs.arrived(sib_k + ARRIVAL.index(place), img_region(*place, 0, ROWS, other=True), me)

    pl.semaphore_wait(barrier, len(img_peers) + len(txt_peers))
    for g in both:
        g.go(10, 0, 5, 11, 1, 6)
    share((0, 0))

    ls = ls_ref[0]
    scale = jnp.exp(jnp.full((1, 256), ls, f32))
    factor = scale * (1.0 / CAP)
    rowacc[...] = jnp.zeros_like(rowacc)
    colacc[...] = jnp.zeros_like(colacc)
    slacc[...] = jnp.zeros_like(slacc)
    posacc[...] = jnp.zeros_like(posacc)

    def rows_of(slot):
        return pl.ds(pl.multiple_of(slot * ROWS, ROWS), ROWS)

    def forward(p, slots):
        t = txt[slots[0]] if len(slots) == 1 else jnp.concatenate([txt[s] for s in slots], axis=0)
        cos = lax.dot_general(t, img[p], (((1,), (1,)), ((), ())), preferred_element_type=f32)
        bent = jnp.tanh(cos * factor)
        power = jnp.exp(CAP * bent)
        held = power * (1.0 - bent * bent)
        for i, s in enumerate(slots):
            here = slice(i * ROWS, (i + 1) * ROWS)
            cosr[p, rows_of(s)] = cos[here]
            hr[p, rows_of(s)] = held[here]
            colacc[s] += power[here, :ROWS] + power[here, ROWS:]
        rowacc[p] += jnp.sum(power.reshape(len(slots) * 16, 8, 256), axis=0)

    def pair_at(i):
        dx = jnp.where((i == 1) | (i == 5), 1, 0) + jnp.where((i == 2) | (i == 6), 3, 0)
        dx = dx + jnp.where((i == 4) | (i == 7), 2, 0)
        dy = jnp.where((i == 3) | (i >= 5), 1, 0)
        return flip(yb, dy) * 4 + turn(x, dx)

    slots = [slot_of(*place) for place in ARRIVAL]

    def batch(first, last, members, unroll=1):
        def body(i, carry):
            forward(pair_at(i), [slots[j] for j in members])
            return carry

        lax.fori_loop(first, last, body, 0, unroll=unroll)

    for g in both:
        g.got(0)
        g.go(2)
        g.got(5)
        g.go(7, 12)
        g.got(10)
        g.go(3, 8)
    for g in both:
        g.got(1)
        g.go(13)
        g.got(6, 11)
    share((1, 0), (3, 0), (0, 1))
    shared((0, 0), (1, 0), (3, 0), (0, 1))
    batch(0, 4, (0, 1, 2, 3))
    for g in both:
        g.got(7)
        g.go(14)
        g.got(2)
    share((2, 0))
    for g in both:
        g.got(3)
        g.go(4)
        g.got(8)
        g.go(9)
    shared((2, 0))
    batch(4, 5, (0, 1, 2, 3))
    gat_i.got(12, 13)
    share((1, 1), (3, 1))
    gat_t.got(12, 13)
    shared((1, 1), (3, 1))
    batch(5, 7, (0, 1, 2, 3))
    batch(0, 7, (4, 5, 6))
    gat_i.got(4, 9, 14)
    share((2, 1))
    gat_t.got(4, 9, 14)
    batch(0, 7, (7,), unroll=7)
    shared((2, 1))
    batch(7, 8, (0, 1, 2, 3))
    batch(7, 8, (4, 5, 6, 7))

    img_me = yb * 8 + x * 2 + c
    txt_me = tb * 4 + z

    def img_index(dx, dy, dc):
        return flip(yb, dy) * 8 + turn(x, dx) * 2 + flip(c, dc)

    rows_all[img_me] = jnp.concatenate([jnp.sum(rowacc[p], axis=0, keepdims=True) for p in range(8)], axis=0)
    k_rows = msgs.take(len(img_peers))
    for i, p in enumerate(img_peers):
        msgs.start(k_rows + i, rows_all.at[img_me], rows_all.at[img_me], img_peer(*p))
    cols_all[txt_me] = jnp.concatenate(
        [jnp.sum(colacc[s].T, axis=0, keepdims=True) for s in range(8)], axis=0
    )
    k_cols = msgs.take(len(txt_peers))
    for i, p in enumerate(txt_peers):
        msgs.start(k_cols + i, cols_all.at[txt_me], cols_all.at[txt_me], txt_peer(*p))

    def collect_img(first, ref):
        for i, (dx, dy, dc) in enumerate(img_peers):
            msgs.arrived(first + i, ref.at[img_index((4 - dx) % 4, dy, dc)], me)

    def collect_txt(first, ref):
        for i, (dz, dy) in enumerate(txt_peers):
            msgs.arrived(first + i, ref.at[slot_of((4 - dz) % 4, dy)], me)

    def add_up(ref, first, last):
        total = ref[first]
        for i in range(first + 1, last):
            total = total + ref[i]
        return total

    collect_txt(k_cols, cols_all)
    col_sum = add_up(cols_all, 0, 8)
    col_weight = (0.5 * scale[:, :ROWS]) / col_sum
    for s in range(8):
        bmat[s] = jnp.broadcast_to(col_weight[s : s + 1], (ROWS, ROWS)).T
    collect_img(k_rows, rows_all)
    row_sum = add_up(rows_all, 0, 16)
    row_weight = (0.5 * scale) / row_sum
    for p in range(8):
        arow[p] = row_weight[p : p + 1]

    lane = lax.broadcasted_iota(jnp.int32, (ROWS, 256), 1)
    diagonal = lane == lax.broadcasted_iota(jnp.int32, (ROWS, 256), 0) + c * ROWS
    pair_mine = (pair_of(0, 0), pair_of(0, 1))

    def grad_tile(p, s, partner_of=None):
        b = bmat[s]
        cos = cosr[p, rows_of(s)]
        g = hr[p, rows_of(s)] * (arow[p] + jnp.concatenate([b, b], axis=1))
        if partner_of is not None:
            slot_blk = jnp.where(s // 4 == tb, y, yq) * 4 + lax.rem(s, 4)
            match = jnp.where(partner_of == slot_blk, 1.0, 0.0).astype(f32)
            partner = jnp.where(diagonal, match, 0.0)
            bent = jnp.tanh(cos * factor)
            g = g - scale * (partner * (1.0 - bent * bent))
            posacc[...] += jnp.sum((CAP * bent * partner).reshape(16, 8, 256), axis=0)
        slacc[...] += jnp.sum((g * cos).reshape(16, 8, 256), axis=0)
        gr[p, rows_of(s)] = g.astype(bf16)

    for dy in range(2):
        partner_of = pairing_ref[(yp if dy else y) * 4 + z]

        def special(s, carry):
            grad_tile(pair_mine[dy], s, partner_of)
            return carry

        lax.fori_loop(0, 8, special, 0)

    def plain(i, carry):
        p = flip(yb, i // 24) * 4 + turn(x, 1 + lax.rem(i // 8, 3))
        grad_tile(p, lax.rem(i, 8))
        return carry

    lax.fori_loop(0, 48, plain, 0, unroll=2)

    sub = lax.broadcasted_iota(jnp.int32, (8, 256), 0)
    half = lax.broadcasted_iota(jnp.int32, (8, 256), 1) // ROWS
    row_part = jnp.where((sub == pair_mine[0]) & (half == c), jnp.log(row_sum), 0.0) - 2.0 * posacc[...]
    col_part = jnp.where(sub[:, :ROWS] == txt_me, jnp.log(col_sum), 0.0)
    slope = slacc[...]
    sc_all[img_me, pl.ds(0, 8)] = row_part[:, :ROWS] + row_part[:, ROWS:] + col_part
    sc_all[img_me, pl.ds(8, 8)] = slope[:, :ROWS] + slope[:, ROWS:]
    k_sc = msgs.take(len(img_peers))
    for i, p in enumerate(img_peers):
        msgs.start(k_sc + i, sc_all.at[img_me], sc_all.at[img_me], img_peer(*p))

    k_sib = msgs.take(8)
    own = pl.ds(pl.multiple_of(c * ROWS, ROWS), ROWS)
    others = pl.ds(pl.multiple_of((1 - c) * ROWS, ROWS), ROWS)

    def img_part(place, low, rows):
        return gi.at[REDUCE.index(place), pl.ds(pl.multiple_of(c * ROWS + low, 32), rows)]

    def txt_part(place, low, rows):
        return gt.at[REDUCE.index(place), pl.ds(low, rows)]

    red_i = Reduce(msgs, img_part, land_i, img_peer(1, 0, 0), img_peer(3, 0, 0), img_peer(0, 1, 0), me)
    red_t = Reduce(msgs, txt_part, land_t, txt_peer(1, 0), txt_peer(3, 0), txt_peer(0, 1), me)
    k_mid = msgs.take(len(txt_peers))

    for i, place in enumerate(REDUCE):
        p, s = pair_of(*place), slot_of(*place)
        gi[i] = lax.dot_general(
            gr[p], txt[...].reshape(8 * ROWS, D), (((0,), (0,)), ((), ())), preferred_element_type=f32
        ).astype(bf16)
        msgs.start(k_sib + i, gi.at[i, others], gi_sib.at[i], sibling)
        lhs = jnp.concatenate([gr[q, rows_of(s)] for q in range(8)], axis=1)
        gt[i] = lax.dot_general(
            lhs, img[...].reshape(16 * ROWS, D), (((1,), (0,)), ((), ())), preferred_element_type=f32
        ).astype(bf16)
        msgs.arrived(k_sib + i, gi_sib.at[i], me)
        gi[i, own] = (gi[i, own].astype(f32) + gi_sib[i].astype(f32)).astype(bf16)
        red_i.step(place)
        red_t.step(place)
        if i == 3:
            collect_img(k_sc, sc_all)
            sc_mid[txt_me] = add_up(sc_all, 0, 16)
            for j, peer in enumerate(txt_peers):
                msgs.start(k_mid + j, sc_mid.at[txt_me], sc_mid.at[txt_me], txt_peer(*peer))

    collect_txt(k_mid, sc_mid)
    totals = add_up(sc_mid, 0, 4) + add_up(sc_mid, 4, 8)
    loss_out[0] = jnp.sum(totals[:8]) * (1.0 / (2.0 * BATCH))
    gls_out[0] = jnp.sum(totals[8:]) * (1.0 / BATCH)

    def back_norm(ref, grad_unit):
        inverse, unit = normalize(ref)
        inner = jnp.sum(unit * grad_unit, axis=1, keepdims=True)
        return inverse * (grad_unit - unit * inner)

    gi_out[...] = back_norm(img_in, red_i.total())
    gt_out[...] = back_norm(txt_in, red_t.total())
    msgs.finish()


N_MSG = 15 + 15 + 8 + 15 + 7 + 15 + 8 + 17 + 17 + 7


def local(image_embed, text_embed, log_scale, pairing):
    vmem, smem = pltpu.VMEM, pltpu.SMEM
    return pl.pallas_call(
        kernel,
        out_shape=[
            jax.ShapeDtypeStruct((ROWS, D), f32),
            jax.ShapeDtypeStruct((ROWS, D), f32),
            jax.ShapeDtypeStruct((1,), f32),
            jax.ShapeDtypeStruct((1,), f32),
        ],
        in_specs=[pl.BlockSpec(memory_space=smem)] * 2 + [pl.BlockSpec(memory_space=vmem)] * 2,
        out_specs=[pl.BlockSpec(memory_space=vmem)] * 2 + [pl.BlockSpec(memory_space=smem)] * 2,
        scratch_shapes=[
            vmem((8, 256, D), bf16),
            vmem((8, ROWS, D), bf16),
            vmem((8, 1024, 256), f32),
            vmem((8, 1024, 256), f32),
            vmem((8, 1024, 256), bf16),
            vmem((8, 8, 256), f32),
            vmem((8, ROWS, ROWS), f32),
            vmem((8, 1, 256), f32),
            vmem((8, ROWS, ROWS), f32),
            vmem((8, 256), f32),
            vmem((8, 256), f32),
            vmem((16, 8, 256), f32),
            vmem((8, 8, ROWS), f32),
            vmem((16, 16, ROWS), f32),
            vmem((8, 16, ROWS), f32),
            vmem((8, 256, D), bf16),
            vmem((8, ROWS, D), bf16),
            vmem((8, ROWS, D), bf16),
            vmem((LAND, D), bf16),
            vmem((LAND, D), bf16),
            pltpu.SemaphoreType.DMA((N_MSG,)),
            pltpu.SemaphoreType.DMA((N_MSG,)),
        ],
        compiler_params=pltpu.CompilerParams(
            collective_id=0, has_side_effects=True, vmem_limit_bytes=60 * 1024 * 1024
        ),
    )(log_scale, pairing, image_embed, text_embed)


def solution(mesh):
    return jax.shard_map(
        local,
        mesh=mesh,
        in_specs=(P(("blk", "grp"), None), P(("blk", "grp"), None), P(), P()),
        out_specs=(P(("blk", "grp"), None), P(("blk", "grp"), None), P(), P()),
        check_vma=False,
    )
```

```python
import jax
import jax.numpy as jnp
from jax import lax
from jax.experimental import pallas as pl
from jax.experimental.pallas import tpu as pltpu
from jax.sharding import PartitionSpec as P

f32, bf16 = jnp.float32, jnp.bfloat16
MESH = pl.DeviceIdType.MESH
CAP = 30.0
ROWS, D, BATCH = 128, 1280, 16384
ARRIVAL = ((0, 0), (1, 0), (3, 0), (0, 1), (2, 0), (1, 1), (3, 1), (2, 1))
REDUCE = ((2, 1), (2, 0), (1, 1), (3, 1), (1, 0), (3, 0), (0, 1), (0, 0))
LAND_AT = (0, 32, 64, 128, 192, 256, 320, 384, 448, 480, 512, 544, 576, 640, 704, 768, 832)
LAND_ROWS = (32, 32, 64, 64, 64, 64, 64, 64, 32, 32, 32, 32, 64, 64, 64, 64, 64)
LAND = 896


def flip(bit, by):
    return bit + by - 2 * bit * by


def turn(place, by):
    return lax.rem(place + by, 4)


class Messages:
    def __init__(self, send, recv):
        self.send, self.recv, self.count, self.open = send, recv, 0, {}

    def take(self, count):
        first = self.count
        self.count += count
        return first

    def start(self, k, src, dst, device):
        copy = pltpu.make_async_remote_copy(
            src, dst, self.send.at[k], self.recv.at[k], device_id=device, device_id_type=MESH
        )
        copy.start()
        self.open[k] = copy

    def arrived(self, k, region, device):
        pltpu.make_async_remote_copy(
            region, region, self.send.at[k], self.recv.at[k], device_id=device, device_id_type=MESH
        ).wait_recv()

    def sent(self, *ks):
        for k in ks:
            self.open.pop(k).wait_send()

    def finish(self):
        self.sent(*list(self.open))


class Gather:
    def __init__(self, msgs, region, plus, minus, pair, me):
        self.m, self.region, self.me = msgs, region, me
        self.plus, self.minus, self.pair = plus, minus, pair
        self.k = msgs.take(15)

    TABLE = (
        ("plus", (0, 0, 0, 64), (3, 0, 0, 64)),
        ("plus", (0, 0, 64, 64), (3, 0, 64, 64)),
        ("plus", (3, 0, 0, 64), (2, 0, 0, 64)),
        ("plus", (0, 1, 0, 64), (3, 1, 0, 64)),
        ("plus", (3, 1, 0, 32), (2, 1, 0, 32)),
        ("minus", (0, 0, 64, 64), (1, 0, 64, 64)),
        ("minus", (0, 0, 0, 64), (1, 0, 0, 64)),
        ("minus", (1, 0, 64, 64), (2, 0, 64, 64)),
        ("minus", (0, 1, 0, 64), (1, 1, 0, 64)),
        ("minus", (1, 1, 32, 32), (2, 1, 32, 32)),
        ("pair", (0, 0, 0, 64), (0, 1, 0, 64)),
        ("pair", (0, 0, 64, 64), (0, 1, 64, 64)),
        ("pair", (1, 0, 64, 64), (1, 1, 64, 64)),
        ("pair", (3, 0, 64, 64), (3, 1, 64, 64)),
        ("pair", (2, 0, 64, 64), (2, 1, 64, 64)),
    )

    def go(self, *ks):
        for k in ks:
            way, here, _ = self.TABLE[k]
            ref = self.region(*here)
            self.m.start(self.k + k, ref, ref, getattr(self, way))

    def sent(self, *ks):
        self.m.sent(*(self.k + k for k in ks))

    def got(self, *ks):
        for k in ks:
            self.m.arrived(self.k + k, self.region(*self.TABLE[k][2]), self.me)


class Reduce:
    TABLE = (
        ("plus", (2, 1), 0, 32),
        ("minus", (2, 1), 32, 32),
        ("pair", (2, 1), 64, 64),
        ("pair", (1, 1), 64, 64),
        ("plus", (1, 1), 0, 64),
        ("pair", (3, 1), 64, 64),
        ("minus", (3, 1), 0, 64),
        ("pair", (0, 1), 64, 64),
        ("plus", (2, 0), 0, 32),
        ("minus", (2, 0), 32, 32),
        ("plus", (2, 0), 64, 32),
        ("minus", (2, 0), 96, 32),
        ("pair", (0, 1), 0, 64),
        ("plus", (1, 0), 0, 64),
        ("plus", (1, 0), 64, 64),
        ("minus", (3, 0), 0, 64),
        ("minus", (3, 0), 64, 64),
    )

    def __init__(self, msgs, part, land, plus, minus, pair, me):
        self.m, self.part, self.land, self.me = msgs, part, land, me
        self.plus, self.minus, self.pair = plus, minus, pair
        self.k = msgs.take(17)

    def where(self, k):
        return self.land.at[pl.ds(LAND_AT[k], LAND_ROWS[k])]

    def go(self, *ks):
        for k in ks:
            way, place, low, rows = self.TABLE[k]
            self.m.start(self.k + k, self.part(place, low, rows), self.where(k), getattr(self, way))

    def sent(self, *ks):
        self.m.sent(*(self.k + k for k in ks))

    def got(self, *ks):
        for k in ks:
            self.m.arrived(self.k + k, self.where(k), self.me)

    def add(self, place, low, rows, *landed):
        ref = self.part(place, low, rows)
        total = ref[...].astype(f32)
        for at in landed:
            total = total + self.land[pl.ds(at, rows)].astype(f32)
        ref[...] = total.astype(bf16)

    def step(self, i):
        if i == 0:
            self.go(0, 1, 2)
        if i == 1:
            self.go(8, 9)
        if i == 3:
            self.got(0)
            self.add((1, 1), 0, 32, LAND_AT[0])
            self.go(4)
            self.got(1)
            self.add((3, 1), 32, 32, LAND_AT[1])
            self.go(6)
            self.sent(2)
            self.go(3)
        if i == 4:
            self.got(2)
            self.add((2, 0), 64, 64, LAND_AT[2])
            self.go(10, 11)
        if i == 5:
            self.got(8)
            self.add((1, 0), 0, 32, LAND_AT[8])
            self.go(13)
            self.got(9)
            self.add((3, 0), 32, 32, LAND_AT[9])
            self.go(15)
        if i == 6:
            self.sent(3)
            self.go(5)

    def last(self):
        self.got(3)
        self.add((1, 0), 64, 64, LAND_AT[3])
        self.got(10)
        self.add((1, 0), 64, 32, LAND_AT[10])
        self.go(14)

    def last_pair(self):
        self.got(4, 6)
        self.add((0, 1), 0, 64, LAND_AT[4], LAND_AT[6])
        self.sent(5)
        self.go(7, 12)

    def last_ring(self):
        self.got(5)
        self.add((3, 0), 64, 64, LAND_AT[5])
        self.got(11)
        self.add((3, 0), 96, 32, LAND_AT[11])
        self.go(16)

    def total(self):
        self.got(13, 15, 12, 7, 14, 16)
        halves = []
        for low, landed in ((0, (13, 15, 12)), (64, (14, 16, 7))):
            total = self.part((0, 0), low, 64)[...].astype(f32)
            for k in landed:
                total = total + self.where(k)[...].astype(f32)
            halves.append(total)
        return jnp.concatenate(halves, axis=0)


def normalize(ref):
    wide = ref[...].astype(f32)
    inverse = lax.rsqrt(jnp.sum(wide * wide, axis=1, keepdims=True) + 1e-06)
    return inverse, wide * inverse


def kernel(
    pairing_ref, ls_ref, img_in, txt_in,
    gi_out, gt_out, sums_out,
    img, img_t, txt, cosr, hr, gr, rowacc, colacc, rowk, colk, arow, bmat, diag, slacc, posacc,
    rows_all, cols_all, sc_all, sc_mid,
    gi, gi_sib, gt, land_i, land_t,
    send, recv,
):
    blk, grp = lax.axis_index("blk"), lax.axis_index("grp")
    x, c, y, z = grp // 2, lax.rem(grp, 2), blk // 4, lax.rem(blk, 4)
    yb = lax.rem(y, 2)
    tb = 1 - yb
    yp = y + 1 - 2 * yb
    yq = lax.rem(y + 3 + 2 * yb, 4)

    def device(x_, y_, z_, c_):
        return (y_ * 4 + z_, x_ * 2 + c_)

    me = device(x, y, z, c)
    sibling = device(x, y, z, 1 - c)
    img_peers = [
        (dx, dy, dc) for dy in range(2) for dx in range(4) for dc in range(2) if (dx, dy, dc) != (0, 0, 0)
    ]
    txt_peers = [(dz, dy) for dy in range(2) for dz in range(4) if (dz, dy) != (0, 0)]

    def img_peer(dx, dy, dc):
        return device(turn(x, dx), yp if dy else y, z, 1 - c if dc else c)

    def txt_peer(dz, dy):
        return device(x, yq if dy else y, turn(z, dz), c)

    barrier = pltpu.get_barrier_semaphore()
    for p in img_peers:
        pl.semaphore_signal(barrier, inc=1, device_id=img_peer(*p), device_id_type=MESH)
    for p in txt_peers:
        pl.semaphore_signal(barrier, inc=1, device_id=txt_peer(*p), device_id_type=MESH)

    def pair_of(dx, dy):
        return flip(yb, dy) * 4 + turn(x, dx)

    def slot_of(dz, dy):
        return flip(tb, dy) * 4 + turn(z, dz)

    def img_region(dx, dy, low, rows, other=False):
        half = 1 - c if other else c
        return img.at[pair_of(dx, dy), pl.ds(pl.multiple_of(half * ROWS + low, 32), rows)]

    def txt_region(dz, dy, low, rows):
        return txt.at[slot_of(dz, dy), pl.ds(low, rows)]

    img_region(0, 0, 0, ROWS)[...] = normalize(img_in)[1].astype(bf16)
    txt_region(0, 0, 0, ROWS)[...] = normalize(txt_in)[1].astype(bf16)

    msgs = Messages(send, recv)
    gat_i = Gather(msgs, img_region, img_peer(1, 0, 0), img_peer(3, 0, 0), img_peer(0, 1, 0), me)
    gat_t = Gather(msgs, txt_region, txt_peer(1, 0), txt_peer(3, 0), txt_peer(0, 1), me)
    both = (gat_i, gat_t)
    sib_k = msgs.take(8)

    def share(*places):
        for place in places:
            ref = img_region(*place, 0, ROWS)
            msgs.start(sib_k + ARRIVAL.index(place), ref, ref, sibling)

    def shared(*places):
        for place in places:
            msgs.arrived(sib_k + ARRIVAL.index(place), img_region(*place, 0, ROWS, other=True), me)

    pl.semaphore_wait(barrier, len(img_peers) + len(txt_peers))
    for g in both:
        g.go(10, 0, 5)
    share((0, 0))

    scale = jnp.exp(jnp.full((1, 256), ls_ref[0], f32))
    factor = scale * (1.0 / CAP)
    for ref in (rowacc, colacc, rowk, colk, slacc, posacc):
        ref[...] = jnp.zeros_like(ref)

    def rows_of(slot):
        return pl.ds(pl.multiple_of(slot * ROWS, ROWS), ROWS)

    def forward(p, s):
        cos = lax.dot_general(txt[s], img_t[p], (((1,), (0,)), ((), ())), preferred_element_type=f32)
        bent = jnp.tanh(cos * factor)
        power = jnp.exp(CAP * bent)
        held = power * (1.0 - bent * bent)
        slope = held * cos
        cosr[p, rows_of(s)] = cos
        hr[p, rows_of(s)] = held
        colacc[s] += power[:, :ROWS] + power[:, ROWS:]
        colk[s] += slope[:, :ROWS] + slope[:, ROWS:]
        rowacc[p] += jnp.sum(power.reshape(16, 8, 256), axis=0)
        rowk[p] += jnp.sum(slope.reshape(16, 8, 256), axis=0)

    def pair_at(i):
        dx = jnp.where((i == 1) | (i == 5), 1, 0) + jnp.where((i == 2) | (i == 6), 3, 0)
        dx = dx + jnp.where((i == 4) | (i == 7), 2, 0)
        dy = jnp.where((i == 3) | (i >= 5), 1, 0)
        return flip(yb, dy) * 4 + turn(x, dx)

    slots = [slot_of(*place) for place in ARRIVAL]

    def batch(first, last, members, unroll=1):
        def body(i, carry):
            for j in members:
                forward(pair_at(i), slots[j])
            return carry

        lax.fori_loop(first, last, body, 0, unroll=unroll)

    def turned(*places):
        shared(*places)
        for place in places:
            p = pair_of(*place)
            img_t[p] = img[p].T

    turned((0, 0))
    for g in both:
        g.sent(10, 0, 5)
        g.go(11, 1, 6)
    batch(0, 1, (0,))
    for g in both:
        g.got(10, 0, 5)
    for g in both:
        g.sent(11, 1, 6)
        g.go(12, 2, 7)
    for g in both:
        g.got(11, 1, 6)
    share((1, 0), (3, 0), (0, 1))
    turned((1, 0), (3, 0), (0, 1))
    batch(0, 1, (1, 2, 3))
    batch(1, 2, (0, 1, 2, 3))
    for g in both:
        g.sent(12, 2, 7)
        g.go(13, 3, 8)
    batch(2, 4, (0, 1, 2, 3))
    for g in both:
        g.got(7)
        g.go(14)
        g.got(2)
    share((2, 0))
    turned((2, 0))
    batch(0, 4, (4,), unroll=4)
    batch(4, 5, (0, 1, 2, 3, 4))
    for g in both:
        g.got(3)
        g.go(4)
        g.got(8)
        g.go(9)
    for g in both:
        g.got(12, 13)
    share((1, 1), (3, 1))
    batch(0, 5, (5, 6))
    turned((1, 1), (3, 1))
    batch(5, 7, (0, 1, 2, 3, 4, 5, 6))
    gat_i.got(4, 9, 14)
    share((2, 1))
    gat_t.got(4, 9, 14)
    batch(0, 7, (7,), unroll=7)
    turned((2, 1))
    batch(7, 8, (0, 1, 2, 3, 4, 5, 6, 7))

    img_me = yb * 8 + x * 2 + c
    txt_me = tb * 4 + z

    def img_index(dx, dy, dc):
        return flip(yb, dy) * 8 + turn(x, dx) * 2 + flip(c, dc)

    rows_all[img_me] = jnp.concatenate([jnp.sum(rowacc[p], axis=0, keepdims=True) for p in range(8)], axis=0)
    k_rows = msgs.take(len(img_peers))
    for i, p in enumerate(img_peers):
        msgs.start(k_rows + i, rows_all.at[img_me], rows_all.at[img_me], img_peer(*p))
    cols_all[txt_me] = jnp.concatenate(
        [jnp.sum(colacc[s].T, axis=0, keepdims=True) for s in range(8)], axis=0
    )
    k_cols = msgs.take(len(txt_peers))
    for i, p in enumerate(txt_peers):
        msgs.start(k_cols + i, cols_all.at[txt_me], cols_all.at[txt_me], txt_peer(*p))

    def collect_img(first, ref):
        for i, (dx, dy, dc) in enumerate(img_peers):
            msgs.arrived(first + i, ref.at[img_index((4 - dx) % 4, dy, dc)], me)

    def collect_txt(first, ref):
        for i, (dz, dy) in enumerate(txt_peers):
            msgs.arrived(first + i, ref.at[slot_of((4 - dz) % 4, dy)], me)

    def add_up(ref, first, last):
        total = ref[first]
        for i in range(first + 1, last):
            total = total + ref[i]
        return total

    lane = lax.broadcasted_iota(jnp.int32, (ROWS, 256), 1)
    diagonal = lane == lax.broadcasted_iota(jnp.int32, (ROWS, 256), 0) + c * ROWS
    pair_mine = (pair_of(0, 0), pair_of(0, 1))

    def matching(s, carry):
        slot_blk = jnp.where(s // 4 == tb, y, yq) * 4 + lax.rem(s, 4)
        for dy in range(2):
            partner_of = pairing_ref[(yp if dy else y) * 4 + z]
            match = jnp.where(partner_of == slot_blk, 1.0, 0.0).astype(f32)
            partner = jnp.where(diagonal, match, 0.0)
            cos = cosr[pair_mine[dy], rows_of(s)]
            bent = jnp.tanh(cos * factor)
            taken = scale * (partner * (1.0 - bent * bent))
            diag[dy, rows_of(s)] = taken
            posacc[...] += jnp.sum((CAP * bent * partner).reshape(16, 8, 256), axis=0)
            slacc[...] += jnp.sum((taken * cos).reshape(16, 8, 256), axis=0)
        return carry

    lax.fori_loop(0, 8, matching, 0, unroll=2)
    row_slope = jnp.concatenate([jnp.sum(rowk[p], axis=0, keepdims=True) for p in range(8)], axis=0)
    col_slope = jnp.concatenate([jnp.sum(colk[s].T, axis=0, keepdims=True) for s in range(8)], axis=0)
    for g in both:
        g.sent(13, 3, 8, 14, 4, 9)
    msgs.sent(*range(sib_k, sib_k + 8))

    collect_txt(k_cols, cols_all)
    col_sum = add_up(cols_all, 0, 8)
    col_weight = (0.5 * scale[:, :ROWS]) / col_sum
    for s in range(8):
        bmat[s] = jnp.broadcast_to(col_weight[s : s + 1], (ROWS, ROWS)).T
    collect_img(k_rows, rows_all)
    row_sum = add_up(rows_all, 0, 16)
    row_weight = (0.5 * scale) / row_sum
    for p in range(8):
        arow[p] = row_weight[p : p + 1]

    def gradient(place):
        p = pair_of(*place)

        def body(s, carry):
            b = bmat[s]
            g = hr[p, rows_of(s)] * (arow[p] + jnp.concatenate([b, b], axis=1))
            if place[0] == 0:
                g = g - diag[place[1], rows_of(s)]
            gr[p, rows_of(s)] = g.astype(bf16)
            return carry

        lax.fori_loop(0, 8, body, 0, unroll=4)

    def send_sums():
        sub = lax.broadcasted_iota(jnp.int32, (8, 256), 0)
        half = lax.broadcasted_iota(jnp.int32, (8, 256), 1) // ROWS
        row_part = jnp.where((sub == pair_mine[0]) & (half == c), jnp.log(row_sum), 0.0) - 2.0 * posacc[...]
        col_part = jnp.where(sub[:, :ROWS] == txt_me, jnp.log(col_sum), 0.0)
        slope = row_weight * row_slope - slacc[...]
        sc_all[img_me, pl.ds(0, 8)] = row_part[:, :ROWS] + row_part[:, ROWS:] + col_part
        sc_all[img_me, pl.ds(8, 8)] = slope[:, :ROWS] + slope[:, ROWS:] + col_weight * col_slope
        for i, p in enumerate(img_peers):
            msgs.start(k_sc + i, sc_all.at[img_me], sc_all.at[img_me], img_peer(*p))

    k_sc = msgs.take(len(img_peers))

    k_sib = msgs.take(8)
    own = pl.ds(pl.multiple_of(c * ROWS, ROWS), ROWS)
    others = pl.ds(pl.multiple_of((1 - c) * ROWS, ROWS), ROWS)

    def img_part(place, low, rows):
        return gi.at[REDUCE.index(place), pl.ds(pl.multiple_of(c * ROWS + low, 32), rows)]

    def txt_part(place, low, rows):
        return gt.at[REDUCE.index(place), pl.ds(low, rows)]

    red_i = Reduce(msgs, img_part, land_i, img_peer(1, 0, 0), img_peer(3, 0, 0), img_peer(0, 1, 0), me)
    red_t = Reduce(msgs, txt_part, land_t, txt_peer(1, 0), txt_peer(3, 0), txt_peer(0, 1), me)
    k_mid = msgs.take(len(txt_peers))

    for i, place in enumerate(REDUCE):
        p, s = pair_of(*place), slot_of(*place)
        if i == 0:
            gradient(place)
        gi[i] = lax.dot_general(
            gr[p], txt[...].reshape(8 * ROWS, D), (((0,), (0,)), ((), ())), preferred_element_type=f32
        ).astype(bf16)
        msgs.start(k_sib + i, gi.at[i, others], gi_sib.at[i], sibling)
        if i == 0:
            for other in REDUCE[1:]:
                gradient(other)
        lhs = jnp.concatenate([gr[q, rows_of(s)] for q in range(8)], axis=1)
        gt[i] = lax.dot_general(
            lhs, img[...].reshape(16 * ROWS, D), (((1,), (0,)), ((), ())), preferred_element_type=f32
        ).astype(bf16)
        msgs.arrived(k_sib + i, gi_sib.at[i], me)
        gi[i, own] = (gi[i, own].astype(f32) + gi_sib[i].astype(f32)).astype(bf16)
        red_i.step(i)
        red_t.step(i)
        if i == 0:
            send_sums()
        if i == 3:
            collect_img(k_sc, sc_all)
            sc_mid[txt_me] = add_up(sc_all, 0, 16)
            for j, peer in enumerate(txt_peers):
                msgs.start(k_mid + j, sc_mid.at[txt_me], sc_mid.at[txt_me], txt_peer(*peer))

    for r in (red_i, red_t):
        r.last()
    for r in (red_i, red_t):
        r.last_pair()
    for r in (red_i, red_t):
        r.last_ring()
    collect_txt(k_mid, sc_mid)
    sums_out[...] = add_up(sc_mid, 0, 4) + add_up(sc_mid, 4, 8)
    for first, count in ((k_rows, 15), (k_cols, 7), (k_sc, 15), (k_mid, 7), (k_sib, 8)):
        msgs.sent(*range(first, first + count))
    gi_out[...] = red_i.total()
    gt_out[...] = red_t.total()
    msgs.finish()


def epilogue(sums, img_in, txt_in, gi_in, gt_in, gi_out, gt_out, loss_out, gls_out):
    def back_norm(ref, grad):
        inverse, unit = normalize(ref)
        grad_unit = grad[...]
        inner = jnp.sum(unit * grad_unit, axis=1, keepdims=True)
        return inverse * (grad_unit - unit * inner)

    gi_out[...] = back_norm(img_in, gi_in)
    gt_out[...] = back_norm(txt_in, gt_in)
    loss_out[0] = jnp.sum(sums[:8]) * (1.0 / (2.0 * BATCH))
    gls_out[0] = jnp.sum(sums[8:]) * (1.0 / BATCH)


N_MSG = 15 + 15 + 8 + 15 + 7 + 15 + 8 + 17 + 17 + 7


def local(image_embed, text_embed, log_scale, pairing):
    vmem, smem = pltpu.VMEM, pltpu.SMEM
    in_vmem, in_smem = pl.BlockSpec(memory_space=vmem), pl.BlockSpec(memory_space=smem)
    grad = jax.ShapeDtypeStruct((ROWS, D), f32)
    scalar = jax.ShapeDtypeStruct((1,), f32)
    unit_img, unit_txt, sums = pl.pallas_call(
        kernel,
        out_shape=[grad, grad, jax.ShapeDtypeStruct((16, ROWS), f32)],
        in_specs=[in_smem] * 2 + [in_vmem] * 2,
        out_specs=[in_vmem] * 3,
        scratch_shapes=[
            vmem((8, 256, D), bf16),
            vmem((8, D, 256), bf16),
            vmem((8, ROWS, D), bf16),
            vmem((8, 1024, 256), f32),
            vmem((8, 1024, 256), f32),
            vmem((8, 1024, 256), bf16),
            vmem((8, 8, 256), f32),
            vmem((8, ROWS, ROWS), f32),
            vmem((8, 8, 256), f32),
            vmem((8, ROWS, ROWS), f32),
            vmem((8, 1, 256), f32),
            vmem((8, ROWS, ROWS), f32),
            vmem((2, 1024, 256), f32),
            vmem((8, 256), f32),
            vmem((8, 256), f32),
            vmem((16, 8, 256), f32),
            vmem((8, 8, ROWS), f32),
            vmem((16, 16, ROWS), f32),
            vmem((8, 16, ROWS), f32),
            vmem((8, 256, D), bf16),
            vmem((8, ROWS, D), bf16),
            vmem((8, ROWS, D), bf16),
            vmem((LAND, D), bf16),
            vmem((LAND, D), bf16),
            pltpu.SemaphoreType.DMA((N_MSG,)),
            pltpu.SemaphoreType.DMA((N_MSG,)),
        ],
        compiler_params=pltpu.CompilerParams(
            collective_id=0, has_side_effects=True, vmem_limit_bytes=60 * 1024 * 1024
        ),
        name="contrast",
    )(pairing, log_scale, image_embed, text_embed)
    return pl.pallas_call(
        epilogue,
        out_shape=[grad, grad, scalar, scalar],
        in_specs=[in_vmem] * 5,
        out_specs=[in_vmem] * 2 + [in_smem] * 2,
        compiler_params=pltpu.CompilerParams(vmem_limit_bytes=60 * 1024 * 1024),
        name="back_norm",
    )(sums, image_embed, text_embed, unit_img, unit_txt)


def solution(mesh):
    return jax.shard_map(
        local,
        mesh=mesh,
        in_specs=(P(("blk", "grp"), None), P(("blk", "grp"), None), P(), P()),
        out_specs=(P(("blk", "grp"), None), P(("blk", "grp"), None), P(), P()),
        check_vma=False,
    )
```

```python
import jax
import jax.numpy as jnp
from jax import lax
from jax.experimental import pallas as pl
from jax.experimental.pallas import tpu as pltpu
from jax.sharding import PartitionSpec as P

f32, bf16 = jnp.float32, jnp.bfloat16
MESH = pl.DeviceIdType.MESH
CAP = 30.0
ROWS, D, BATCH = 128, 1280, 16384
ARRIVAL = ((0, 0), (1, 0), (3, 0), (0, 1), (2, 0), (1, 1), (3, 1), (2, 1))
REDUCE = ((2, 1), (2, 0), (1, 1), (3, 1), (1, 0), (3, 0), (0, 1), (0, 0))
LAND_AT = (0, 32, 64, 128, 192, 256, 320, 384, 448, 480, 512, 544, 576, 640, 704, 768, 832)
LAND_ROWS = (32, 32, 64, 64, 64, 64, 64, 64, 32, 32, 32, 32, 64, 64, 64, 64, 64)
LAND = 896


def flip(bit, by):
    return bit + by - 2 * bit * by


def turn(place, by):
    return lax.rem(place + by, 4)


class Messages:
    def __init__(self, send, recv):
        self.send, self.recv, self.count, self.open = send, recv, 0, {}

    def take(self, count):
        first = self.count
        self.count += count
        return first

    def start(self, k, src, dst, device):
        copy = pltpu.make_async_remote_copy(
            src, dst, self.send.at[k], self.recv.at[k], device_id=device, device_id_type=MESH
        )
        copy.start()
        self.open[k] = copy

    def arrived(self, k, region, device):
        pltpu.make_async_remote_copy(
            region, region, self.send.at[k], self.recv.at[k], device_id=device, device_id_type=MESH
        ).wait_recv()

    def sent(self, *ks):
        for k in ks:
            self.open.pop(k).wait_send()

    def finish(self):
        self.sent(*list(self.open))


class Gather:
    def __init__(self, msgs, region, plus, minus, pair, me):
        self.m, self.region, self.me = msgs, region, me
        self.plus, self.minus, self.pair = plus, minus, pair
        self.k = msgs.take(17)

    TABLE = (
        ("plus", (0, 0, 0, 64), (3, 0, 0, 64)),
        ("plus", (0, 0, 64, 64), (3, 0, 64, 64)),
        ("plus", (3, 0, 0, 64), (2, 0, 0, 64)),
        ("plus", (0, 1, 0, 32), (3, 1, 0, 32)),
        ("plus", (3, 1, 0, 32), (2, 1, 0, 32)),
        ("minus", (0, 0, 64, 64), (1, 0, 64, 64)),
        ("minus", (0, 0, 0, 64), (1, 0, 0, 64)),
        ("minus", (1, 0, 64, 64), (2, 0, 64, 64)),
        ("minus", (0, 1, 32, 32), (1, 1, 32, 32)),
        ("minus", (1, 1, 32, 32), (2, 1, 32, 32)),
        ("pair", (0, 0, 0, 64), (0, 1, 0, 64)),
        ("pair", (0, 0, 64, 64), (0, 1, 64, 64)),
        ("pair", (1, 0, 64, 64), (1, 1, 64, 64)),
        ("pair", (3, 0, 64, 64), (3, 1, 64, 64)),
        ("pair", (2, 0, 64, 64), (2, 1, 64, 64)),
        ("plus", (0, 1, 32, 32), (3, 1, 32, 32)),
        ("minus", (0, 1, 0, 32), (1, 1, 0, 32)),
    )

    def go(self, *ks):
        for k in ks:
            way, here, _ = self.TABLE[k]
            ref = self.region(*here)
            self.m.start(self.k + k, ref, ref, getattr(self, way))

    def sent(self, *ks):
        self.m.sent(*(self.k + k for k in ks))

    def got(self, *ks):
        for k in ks:
            self.m.arrived(self.k + k, self.region(*self.TABLE[k][2]), self.me)


class Reduce:
    TABLE = (
        ("plus", (2, 1), 0, 32),
        ("minus", (2, 1), 32, 32),
        ("pair", (2, 1), 64, 64),
        ("pair", (1, 1), 64, 64),
        ("plus", (1, 1), 0, 64),
        ("pair", (3, 1), 64, 64),
        ("minus", (3, 1), 0, 64),
        ("pair", (0, 1), 64, 64),
        ("plus", (2, 0), 0, 32),
        ("minus", (2, 0), 32, 32),
        ("plus", (2, 0), 64, 32),
        ("minus", (2, 0), 96, 32),
        ("pair", (0, 1), 0, 64),
        ("plus", (1, 0), 0, 64),
        ("plus", (1, 0), 64, 64),
        ("minus", (3, 0), 0, 64),
        ("minus", (3, 0), 64, 64),
    )

    def __init__(self, msgs, part, land, plus, minus, pair, me):
        self.m, self.part, self.land, self.me = msgs, part, land, me
        self.plus, self.minus, self.pair = plus, minus, pair
        self.k = msgs.take(17)

    def where(self, k):
        return self.land.at[pl.ds(LAND_AT[k], LAND_ROWS[k])]

    def go(self, *ks):
        for k in ks:
            way, place, low, rows = self.TABLE[k]
            self.m.start(self.k + k, self.part(place, low, rows), self.where(k), getattr(self, way))

    def sent(self, *ks):
        self.m.sent(*(self.k + k for k in ks))

    def got(self, *ks):
        for k in ks:
            self.m.arrived(self.k + k, self.where(k), self.me)

    def add(self, place, low, rows, *landed):
        ref = self.part(place, low, rows)
        total = ref[...].astype(f32)
        for at in landed:
            total = total + self.land[pl.ds(at, rows)].astype(f32)
        ref[...] = total.astype(bf16)

    def step(self, i):
        if i == 0:
            self.go(0, 1, 2)
        if i == 1:
            self.go(8, 9)
        if i == 2:
            self.go(3)
            self.got(0)
            self.add((1, 1), 0, 32, LAND_AT[0])
            self.go(4)
        if i == 3:
            self.go(5)
            self.got(1)
            self.add((3, 1), 32, 32, LAND_AT[1])
            self.go(6)
        if i == 4:
            self.got(2)
            self.add((2, 0), 64, 64, LAND_AT[2])
            self.go(10, 11)
            self.got(8)
            self.add((1, 0), 0, 32, LAND_AT[8])
            self.go(13)
        if i == 5:
            self.got(9)
            self.add((3, 0), 32, 32, LAND_AT[9])
            self.go(15)
        if i == 6:
            self.go(7)

    def last(self):
        self.got(4, 6)
        self.add((0, 1), 0, 64, LAND_AT[4], LAND_AT[6])
        self.go(12)
        self.got(3)
        self.add((1, 0), 64, 64, LAND_AT[3])
        self.got(10)
        self.add((1, 0), 64, 32, LAND_AT[10])
        self.go(14)

    def last_ring(self):
        self.got(5)
        self.add((3, 0), 64, 64, LAND_AT[5])
        self.got(11)
        self.add((3, 0), 96, 32, LAND_AT[11])
        self.go(16)

    def total(self):
        self.got(13, 15, 12, 7, 14, 16)
        halves = []
        for low, landed in ((0, (13, 15, 12)), (64, (14, 16, 7))):
            total = self.part((0, 0), low, 64)[...].astype(f32)
            for k in landed:
                total = total + self.where(k)[...].astype(f32)
            halves.append(total)
        return jnp.concatenate(halves, axis=0)


def normalize(ref):
    wide = ref[...].astype(f32)
    inverse = lax.rsqrt(jnp.sum(wide * wide, axis=1, keepdims=True) + 1e-06)
    return inverse, wide * inverse


def kernel(
    pairing_ref, ls_ref, img_in, txt_in,
    gi_out, gt_out, sums_out,
    img, img_t, txt, cosr, hr, gr, rowacc, colacc, rowk, colk, arow, bmat, diag, slacc, posacc,
    rows_all, cols_all, sc_all, sc_mid,
    gi, gi_sib, gt, land_i, land_t,
    send, recv,
):
    blk, grp = lax.axis_index("blk"), lax.axis_index("grp")
    x, c, y, z = grp // 2, lax.rem(grp, 2), blk // 4, lax.rem(blk, 4)
    yb = lax.rem(y, 2)
    tb = 1 - yb
    yp = y + 1 - 2 * yb
    yq = lax.rem(y + 3 + 2 * yb, 4)

    def device(x_, y_, z_, c_):
        return (y_ * 4 + z_, x_ * 2 + c_)

    me = device(x, y, z, c)
    sibling = device(x, y, z, 1 - c)
    img_peers = [
        (dx, dy, dc) for dy in range(2) for dx in range(4) for dc in range(2) if (dx, dy, dc) != (0, 0, 0)
    ]
    txt_peers = [(dz, dy) for dy in range(2) for dz in range(4) if (dz, dy) != (0, 0)]

    def img_peer(dx, dy, dc):
        return device(turn(x, dx), yp if dy else y, z, 1 - c if dc else c)

    def txt_peer(dz, dy):
        return device(x, yq if dy else y, turn(z, dz), c)

    barrier = pltpu.get_barrier_semaphore()
    for p in img_peers:
        pl.semaphore_signal(barrier, inc=1, device_id=img_peer(*p), device_id_type=MESH)
    for p in txt_peers:
        pl.semaphore_signal(barrier, inc=1, device_id=txt_peer(*p), device_id_type=MESH)

    def pair_of(dx, dy):
        return flip(yb, dy) * 4 + turn(x, dx)

    def slot_of(dz, dy):
        return flip(tb, dy) * 4 + turn(z, dz)

    def img_region(dx, dy, low, rows, other=False):
        half = 1 - c if other else c
        return img.at[pair_of(dx, dy), pl.ds(pl.multiple_of(half * ROWS + low, 32), rows)]

    def txt_region(dz, dy, low, rows):
        return txt.at[slot_of(dz, dy), pl.ds(low, rows)]

    img_region(0, 0, 0, ROWS)[...] = normalize(img_in)[1].astype(bf16)
    txt_region(0, 0, 0, ROWS)[...] = normalize(txt_in)[1].astype(bf16)

    msgs = Messages(send, recv)
    gat_i = Gather(msgs, img_region, img_peer(1, 0, 0), img_peer(3, 0, 0), img_peer(0, 1, 0), me)
    gat_t = Gather(msgs, txt_region, txt_peer(1, 0), txt_peer(3, 0), txt_peer(0, 1), me)
    both = (gat_i, gat_t)
    sib_k = msgs.take(9)

    def pieces(places):
        for place in places:
            if place == (2, 1):
                yield sib_k + 7, (*place, 0, 64)
                yield sib_k + 8, (*place, 64, 64)
            else:
                yield sib_k + ARRIVAL.index(place), (*place, 0, ROWS)

    def share(*places, only=(0, 1)):
        for i, (k, piece) in enumerate(pieces(places)):
            if i in only or len(places) > 1:
                ref = img_region(*piece)
                msgs.start(k, ref, ref, sibling)

    def shared(*places):
        for k, piece in pieces(places):
            msgs.arrived(k, img_region(*piece, other=True), me)

    pl.semaphore_wait(barrier, len(img_peers) + len(txt_peers))
    for g in both:
        g.go(10, 0, 5, 11, 1, 6)
    share((0, 0))

    scale = jnp.exp(jnp.full((1, 256), ls_ref[0], f32))
    factor = scale * (1.0 / CAP)
    for ref in (rowacc, colacc, rowk, colk, slacc, posacc):
        ref[...] = jnp.zeros_like(ref)

    def rows_of(slot):
        return pl.ds(pl.multiple_of(slot * ROWS, ROWS), ROWS)

    def forward(p, s):
        cos = lax.dot_general(txt[s], img_t[p], (((1,), (0,)), ((), ())), preferred_element_type=f32)
        bent = jnp.tanh(cos * factor)
        power = jnp.exp(CAP * bent)
        held = power * (1.0 - bent * bent)
        slope = held * cos
        cosr[p, rows_of(s)] = cos
        hr[p, rows_of(s)] = held
        colacc[s] += power[:, :ROWS] + power[:, ROWS:]
        colk[s] += slope[:, :ROWS] + slope[:, ROWS:]
        rowacc[p] += jnp.sum(power.reshape(16, 8, 256), axis=0)
        rowk[p] += jnp.sum(slope.reshape(16, 8, 256), axis=0)

    def pair_at(i):
        dx = jnp.where((i == 1) | (i == 5), 1, 0) + jnp.where((i == 2) | (i == 6), 3, 0)
        dx = dx + jnp.where((i == 4) | (i == 7), 2, 0)
        dy = jnp.where((i == 3) | (i >= 5), 1, 0)
        return flip(yb, dy) * 4 + turn(x, dx)

    slots = [slot_of(*place) for place in ARRIVAL]

    def batch(first, last, members, unroll=1):
        def body(i, carry):
            for j in members:
                forward(pair_at(i), slots[j])
            return carry

        lax.fori_loop(first, last, body, 0, unroll=unroll)

    def turned(*places):
        shared(*places)
        for place in places:
            p = pair_of(*place)
            img_t[p] = img[p].T

    turned((0, 0))
    batch(0, 1, (0,))
    for g in both:
        g.got(0, 5, 10)
        g.go(2, 7, 12, 3, 8, 15, 16)
    for g in both:
        g.got(1)
        g.go(13)
        g.got(6, 11)
    share((1, 0), (3, 0), (0, 1))
    batch(0, 1, (1, 2, 3))
    turned((1, 0), (3, 0), (0, 1))
    batch(1, 4, (0, 1, 2, 3))
    for g in both:
        g.got(7)
        g.go(14)
        g.got(2)
    share((2, 0))
    batch(0, 4, (4,), unroll=4)
    for g in both:
        g.got(3)
        g.go(4)
        g.got(8)
        g.go(9)
    turned((2, 0))
    batch(4, 5, (0, 1, 2, 3, 4))
    gat_i.got(12, 13, 15, 16)
    share((1, 1), (3, 1))
    gat_t.got(12, 13, 15, 16)
    batch(0, 5, (5, 6))
    turned((1, 1), (3, 1))
    batch(5, 6, (0, 1, 2, 3, 4, 5, 6))
    gat_i.got(4, 9)
    share((2, 1), only=(0,))
    batch(6, 7, (0, 1, 2, 3, 4, 5, 6))
    gat_i.got(14)
    share((2, 1), only=(1,))
    gat_t.got(4, 9, 14)
    batch(0, 7, (7,), unroll=7)
    turned((2, 1))
    batch(7, 8, (0, 1, 2, 3, 4, 5, 6, 7))

    img_me = yb * 8 + x * 2 + c
    txt_me = tb * 4 + z

    def img_index(dx, dy, dc):
        return flip(yb, dy) * 8 + turn(x, dx) * 2 + flip(c, dc)

    rows_all[img_me] = jnp.concatenate([jnp.sum(rowacc[p], axis=0, keepdims=True) for p in range(8)], axis=0)
    k_rows = msgs.take(len(img_peers))
    for i, p in enumerate(img_peers):
        msgs.start(k_rows + i, rows_all.at[img_me], rows_all.at[img_me], img_peer(*p))
    cols_all[txt_me] = jnp.concatenate(
        [jnp.sum(colacc[s].T, axis=0, keepdims=True) for s in range(8)], axis=0
    )
    k_cols = msgs.take(len(txt_peers))
    for i, p in enumerate(txt_peers):
        msgs.start(k_cols + i, cols_all.at[txt_me], cols_all.at[txt_me], txt_peer(*p))

    def collect_img(first, ref):
        for i, (dx, dy, dc) in enumerate(img_peers):
            msgs.arrived(first + i, ref.at[img_index((4 - dx) % 4, dy, dc)], me)

    def collect_txt(first, ref):
        for i, (dz, dy) in enumerate(txt_peers):
            msgs.arrived(first + i, ref.at[slot_of((4 - dz) % 4, dy)], me)

    def add_up(ref, first, last):
        total = ref[first]
        for i in range(first + 1, last):
            total = total + ref[i]
        return total

    lane = lax.broadcasted_iota(jnp.int32, (ROWS, 256), 1)
    diagonal = lane == lax.broadcasted_iota(jnp.int32, (ROWS, 256), 0) + c * ROWS
    pair_mine = (pair_of(0, 0), pair_of(0, 1))

    def matching(s, carry):
        slot_blk = jnp.where(s // 4 == tb, y, yq) * 4 + lax.rem(s, 4)
        for dy in range(2):
            partner_of = pairing_ref[(yp if dy else y) * 4 + z]
            match = jnp.where(partner_of == slot_blk, 1.0, 0.0).astype(f32)
            partner = jnp.where(diagonal, match, 0.0)
            cos = cosr[pair_mine[dy], rows_of(s)]
            bent = jnp.tanh(cos * factor)
            taken = scale * (partner * (1.0 - bent * bent))
            diag[dy, rows_of(s)] = taken
            posacc[...] += jnp.sum((CAP * bent * partner).reshape(16, 8, 256), axis=0)
            slacc[...] += jnp.sum((taken * cos).reshape(16, 8, 256), axis=0)
        return carry

    lax.fori_loop(0, 8, matching, 0, unroll=2)
    row_slope = jnp.concatenate([jnp.sum(rowk[p], axis=0, keepdims=True) for p in range(8)], axis=0)
    col_slope = jnp.concatenate([jnp.sum(colk[s].T, axis=0, keepdims=True) for s in range(8)], axis=0)
    for g in both:
        g.sent(*range(17))
    msgs.sent(*range(sib_k, sib_k + 9))

    collect_txt(k_cols, cols_all)
    col_sum = add_up(cols_all, 0, 8)
    col_weight = (0.5 * scale[:, :ROWS]) / col_sum
    for s in range(8):
        bmat[s] = jnp.broadcast_to(col_weight[s : s + 1], (ROWS, ROWS)).T
    collect_img(k_rows, rows_all)
    row_sum = add_up(rows_all, 0, 16)
    row_weight = (0.5 * scale) / row_sum
    for p in range(8):
        arow[p] = row_weight[p : p + 1]

    def gradient(place):
        p = pair_of(*place)

        def body(s, carry):
            b = bmat[s]
            g = hr[p, rows_of(s)] * (arow[p] + jnp.concatenate([b, b], axis=1))
            if place[0] == 0:
                g = g - diag[place[1], rows_of(s)]
            gr[p, rows_of(s)] = g.astype(bf16)
            return carry

        lax.fori_loop(0, 8, body, 0, unroll=4)

    def send_sums():
        sub = lax.broadcasted_iota(jnp.int32, (8, 256), 0)
        half = lax.broadcasted_iota(jnp.int32, (8, 256), 1) // ROWS
        row_part = jnp.where((sub == pair_mine[0]) & (half == c), jnp.log(row_sum), 0.0) - 2.0 * posacc[...]
        col_part = jnp.where(sub[:, :ROWS] == txt_me, jnp.log(col_sum), 0.0)
        slope = row_weight * row_slope - slacc[...]
        sc_all[img_me, pl.ds(0, 8)] = row_part[:, :ROWS] + row_part[:, ROWS:] + col_part
        sc_all[img_me, pl.ds(8, 8)] = slope[:, :ROWS] + slope[:, ROWS:] + col_weight * col_slope
        for i, p in enumerate(img_peers):
            msgs.start(k_sc + i, sc_all.at[img_me], sc_all.at[img_me], img_peer(*p))

    k_sc = msgs.take(len(img_peers))

    k_sib = msgs.take(8)
    own = pl.ds(pl.multiple_of(c * ROWS, ROWS), ROWS)
    others = pl.ds(pl.multiple_of((1 - c) * ROWS, ROWS), ROWS)

    def img_part(place, low, rows):
        return gi.at[REDUCE.index(place), pl.ds(pl.multiple_of(c * ROWS + low, 32), rows)]

    def txt_part(place, low, rows):
        return gt.at[REDUCE.index(place), pl.ds(low, rows)]

    red_i = Reduce(msgs, img_part, land_i, img_peer(1, 0, 0), img_peer(3, 0, 0), img_peer(0, 1, 0), me)
    red_t = Reduce(msgs, txt_part, land_t, txt_peer(1, 0), txt_peer(3, 0), txt_peer(0, 1), me)
    k_mid = msgs.take(len(txt_peers))

    def img_product(i):
        gi[i] = lax.dot_general(
            gr[pair_of(*REDUCE[i])], txt[...].reshape(8 * ROWS, D), (((0,), (0,)), ((), ())), preferred_element_type=f32
        ).astype(bf16)
        msgs.start(k_sib + i, gi.at[i, others], gi_sib.at[i], sibling)

    def img_send(i):
        msgs.arrived(k_sib + i, gi_sib.at[i], me)
        gi[i, own] = (gi[i, own].astype(f32) + gi_sib[i].astype(f32)).astype(bf16)
        red_i.step(i)

    def txt_product(i):
        s = slot_of(*REDUCE[i])
        lhs = jnp.concatenate([gr[q, rows_of(s)] for q in range(8)], axis=1)
        gt[i] = lax.dot_general(
            lhs, img[...].reshape(16 * ROWS, D), (((1,), (0,)), ((), ())), preferred_element_type=f32
        ).astype(bf16)
        red_t.step(i)

    gradient(REDUCE[0])
    img_product(0)
    for place in REDUCE[1:]:
        gradient(place)
    img_send(0)
    txt_product(0)
    send_sums()
    for i in range(1, 8):
        img_product(i)
        if i > 1:
            img_send(i - 1)
        txt_product(i)
        if i == 3:
            collect_img(k_sc, sc_all)
            sc_mid[txt_me] = add_up(sc_all, 0, 16)
            for j, peer in enumerate(txt_peers):
                msgs.start(k_mid + j, sc_mid.at[txt_me], sc_mid.at[txt_me], txt_peer(*peer))
    img_send(7)
    for r in (red_i, red_t):
        r.last()
    for r in (red_i, red_t):
        r.last_ring()
    collect_txt(k_mid, sc_mid)
    sums_out[...] = add_up(sc_mid, 0, 4) + add_up(sc_mid, 4, 8)
    for first, count in ((k_rows, 15), (k_cols, 7), (k_sc, 15), (k_mid, 7), (k_sib, 8)):
        msgs.sent(*range(first, first + count))
    gi_out[...] = red_i.total()
    gt_out[...] = red_t.total()
    msgs.finish()


def epilogue(sums, img_in, txt_in, gi_in, gt_in, gi_out, gt_out, loss_out, gls_out):
    def back_norm(ref, grad):
        inverse, unit = normalize(ref)
        grad_unit = grad[...]
        inner = jnp.sum(unit * grad_unit, axis=1, keepdims=True)
        return inverse * (grad_unit - unit * inner)

    gi_out[...] = back_norm(img_in, gi_in)
    gt_out[...] = back_norm(txt_in, gt_in)
    loss_out[0] = jnp.sum(sums[:8]) * (1.0 / (2.0 * BATCH))
    gls_out[0] = jnp.sum(sums[8:]) * (1.0 / BATCH)


N_MSG = 17 + 17 + 9 + 15 + 7 + 15 + 8 + 17 + 17 + 7


def local(image_embed, text_embed, log_scale, pairing):
    vmem, smem = pltpu.VMEM, pltpu.SMEM
    in_vmem, in_smem = pl.BlockSpec(memory_space=vmem), pl.BlockSpec(memory_space=smem)
    grad = jax.ShapeDtypeStruct((ROWS, D), f32)
    scalar = jax.ShapeDtypeStruct((1,), f32)
    unit_img, unit_txt, sums = pl.pallas_call(
        kernel,
        out_shape=[grad, grad, jax.ShapeDtypeStruct((16, ROWS), f32)],
        in_specs=[in_smem] * 2 + [in_vmem] * 2,
        out_specs=[in_vmem] * 3,
        scratch_shapes=[
            vmem((8, 256, D), bf16),
            vmem((8, D, 256), bf16),
            vmem((8, ROWS, D), bf16),
            vmem((8, 1024, 256), f32),
            vmem((8, 1024, 256), f32),
            vmem((8, 1024, 256), bf16),
            vmem((8, 8, 256), f32),
            vmem((8, ROWS, ROWS), f32),
            vmem((8, 8, 256), f32),
            vmem((8, ROWS, ROWS), f32),
            vmem((8, 1, 256), f32),
            vmem((8, ROWS, ROWS), f32),
            vmem((2, 1024, 256), f32),
            vmem((8, 256), f32),
            vmem((8, 256), f32),
            vmem((16, 8, 256), f32),
            vmem((8, 8, ROWS), f32),
            vmem((16, 16, ROWS), f32),
            vmem((8, 16, ROWS), f32),
            vmem((8, 256, D), bf16),
            vmem((8, ROWS, D), bf16),
            vmem((8, ROWS, D), bf16),
            vmem((LAND, D), bf16),
            vmem((LAND, D), bf16),
            pltpu.SemaphoreType.DMA((N_MSG,)),
            pltpu.SemaphoreType.DMA((N_MSG,)),
        ],
        compiler_params=pltpu.CompilerParams(
            collective_id=0, has_side_effects=True, vmem_limit_bytes=60 * 1024 * 1024
        ),
        name="contrast",
    )(pairing, log_scale, image_embed, text_embed)
    return pl.pallas_call(
        epilogue,
        out_shape=[grad, grad, scalar, scalar],
        in_specs=[in_vmem] * 5,
        out_specs=[in_vmem] * 2 + [in_smem] * 2,
        compiler_params=pltpu.CompilerParams(vmem_limit_bytes=60 * 1024 * 1024),
        name="back_norm",
    )(sums, image_embed, text_embed, unit_img, unit_txt)


def solution(mesh):
    return jax.shard_map(
        local,
        mesh=mesh,
        in_specs=(P(("blk", "grp"), None), P(("blk", "grp"), None), P(), P()),
        out_specs=(P(("blk", "grp"), None), P(("blk", "grp"), None), P(), P()),
        check_vma=False,
    )
```

```python
import jax
import jax.numpy as jnp
from jax import lax
from jax.experimental import pallas as pl
from jax.experimental.pallas import tpu as pltpu
from jax.sharding import PartitionSpec as P

f32, bf16 = jnp.float32, jnp.bfloat16
MESH = pl.DeviceIdType.MESH
CAP = 30.0
ROWS, D, BATCH = 128, 1280, 16384
ARRIVAL = ((0, 0), (1, 0), (3, 0), (0, 1), (2, 0), (1, 1), (3, 1), (2, 1))
REDUCE = ((2, 1), (2, 0), (1, 1), (3, 1), (1, 0), (3, 0), (0, 1), (0, 0))
LAND_AT = (0, 32, 64, 128, 192, 256, 320, 384, 448, 480, 512, 544, 576, 640, 704, 768, 832)
LAND_ROWS = (32, 32, 64, 64, 64, 64, 64, 64, 32, 32, 32, 32, 64, 64, 64, 64, 64)
LAND = 896


def flip(bit, by):
    return bit + by - 2 * bit * by


def turn(place, by):
    return lax.rem(place + by, 4)


class Messages:
    def __init__(self, send, recv):
        self.send, self.recv, self.count, self.open = send, recv, 0, {}

    def take(self, count):
        first = self.count
        self.count += count
        return first

    def start(self, k, src, dst, device):
        copy = pltpu.make_async_remote_copy(
            src, dst, self.send.at[k], self.recv.at[k], device_id=device, device_id_type=MESH
        )
        copy.start()
        self.open[k] = copy

    def arrived(self, k, region, device):
        pltpu.make_async_remote_copy(
            region, region, self.send.at[k], self.recv.at[k], device_id=device, device_id_type=MESH
        ).wait_recv()

    def sent(self, *ks):
        for k in ks:
            self.open.pop(k).wait_send()

    def finish(self):
        self.sent(*list(self.open))


class Gather:
    def __init__(self, msgs, region, plus, minus, pair, me):
        self.m, self.region, self.me = msgs, region, me
        self.plus, self.minus, self.pair = plus, minus, pair
        self.k = msgs.take(17)

    TABLE = (
        ("plus", (0, 0, 0, 64), (3, 0, 0, 64)),
        ("plus", (0, 0, 64, 64), (3, 0, 64, 64)),
        ("plus", (3, 0, 0, 64), (2, 0, 0, 64)),
        ("plus", (0, 1, 0, 32), (3, 1, 0, 32)),
        ("plus", (3, 1, 0, 32), (2, 1, 0, 32)),
        ("minus", (0, 0, 64, 64), (1, 0, 64, 64)),
        ("minus", (0, 0, 0, 64), (1, 0, 0, 64)),
        ("minus", (1, 0, 64, 64), (2, 0, 64, 64)),
        ("minus", (0, 1, 32, 32), (1, 1, 32, 32)),
        ("minus", (1, 1, 32, 32), (2, 1, 32, 32)),
        ("pair", (0, 0, 0, 64), (0, 1, 0, 64)),
        ("pair", (0, 0, 64, 64), (0, 1, 64, 64)),
        ("pair", (1, 0, 64, 64), (1, 1, 64, 64)),
        ("pair", (3, 0, 64, 64), (3, 1, 64, 64)),
        ("pair", (2, 0, 64, 64), (2, 1, 64, 64)),
        ("plus", (0, 1, 32, 32), (3, 1, 32, 32)),
        ("minus", (0, 1, 0, 32), (1, 1, 0, 32)),
    )

    def go(self, *ks):
        for k in ks:
            way, here, _ = self.TABLE[k]
            ref = self.region(*here)
            self.m.start(self.k + k, ref, ref, getattr(self, way))

    def sent(self, *ks):
        self.m.sent(*(self.k + k for k in ks))

    def got(self, *ks):
        for k in ks:
            self.m.arrived(self.k + k, self.region(*self.TABLE[k][2]), self.me)


class Reduce:
    TABLE = (
        ("plus", (2, 1), 0, 32),
        ("minus", (2, 1), 32, 32),
        ("pair", (2, 1), 64, 64),
        ("pair", (1, 1), 64, 64),
        ("plus", (1, 1), 0, 64),
        ("pair", (3, 1), 64, 64),
        ("minus", (3, 1), 0, 64),
        ("pair", (0, 1), 64, 64),
        ("plus", (2, 0), 0, 32),
        ("minus", (2, 0), 32, 32),
        ("plus", (2, 0), 64, 32),
        ("minus", (2, 0), 96, 32),
        ("pair", (0, 1), 0, 64),
        ("plus", (1, 0), 0, 64),
        ("plus", (1, 0), 64, 64),
        ("minus", (3, 0), 0, 64),
        ("minus", (3, 0), 64, 64),
    )

    def __init__(self, msgs, part, land, plus, minus, pair, me):
        self.m, self.part, self.land, self.me = msgs, part, land, me
        self.plus, self.minus, self.pair = plus, minus, pair
        self.k = msgs.take(17)

    def where(self, k):
        return self.land.at[pl.ds(LAND_AT[k], LAND_ROWS[k])]

    def go(self, *ks):
        for k in ks:
            way, place, low, rows = self.TABLE[k]
            self.m.start(self.k + k, self.part(place, low, rows), self.where(k), getattr(self, way))

    def sent(self, *ks):
        self.m.sent(*(self.k + k for k in ks))

    def got(self, *ks):
        for k in ks:
            self.m.arrived(self.k + k, self.where(k), self.me)

    def add(self, place, low, rows, *landed):
        ref = self.part(place, low, rows)
        total = ref[...].astype(f32)
        for at in landed:
            total = total + self.land[pl.ds(at, rows)].astype(f32)
        ref[...] = total.astype(bf16)

    def step(self, i):
        if i == 0:
            self.go(0, 1, 2)
        if i == 1:
            self.go(8, 9)
        if i == 2:
            self.go(3)
            self.got(0)
            self.add((1, 1), 0, 32, LAND_AT[0])
            self.go(4)
        if i == 3:
            self.go(5)
            self.got(1)
            self.add((3, 1), 32, 32, LAND_AT[1])
            self.go(6)
        if i == 4:
            self.got(2)
            self.add((2, 0), 64, 64, LAND_AT[2])
            self.go(10, 11)
            self.got(8)
            self.add((1, 0), 0, 32, LAND_AT[8])
            self.go(13)
        if i == 5:
            self.got(9)
            self.add((3, 0), 32, 32, LAND_AT[9])
            self.go(15)
        if i == 6:
            self.go(7)

    def last(self):
        self.got(4, 6)
        self.add((0, 1), 0, 64, LAND_AT[4], LAND_AT[6])
        self.go(12)
        self.got(3)
        self.add((1, 0), 64, 64, LAND_AT[3])
        self.got(10)
        self.add((1, 0), 64, 32, LAND_AT[10])
        self.go(14)

    def last_ring(self):
        self.got(5)
        self.add((3, 0), 64, 64, LAND_AT[5])
        self.got(11)
        self.add((3, 0), 96, 32, LAND_AT[11])
        self.go(16)

    def total(self, low, *ks):
        self.got(*ks)
        total = self.part((0, 0), low, 64)[...].astype(f32)
        for k in ks:
            total = total + self.where(k)[...].astype(f32)
        return total


def normalize(embed):
    wide = embed.astype(f32)
    inverse = lax.rsqrt(jnp.sum(wide * wide, axis=1, keepdims=True) + 1e-06)
    return inverse, wide * inverse


def kernel(
    ls_ref, pairing_in, img_in, txt_in,
    gi_out, gt_out, sums_out,
    img, img_t, txt, cosr, hr, gr, rowacc, colacc, rowk, colk, arow, bmat, diag, slacc, posacc,
    rows_all, cols_all, sc_all, sc_mid,
    gi, gi_sib, gt, land_i, land_t,
    pairing_ref, embeds, units, sums, own_sem, send, recv,
):
    blk, grp = lax.axis_index("blk"), lax.axis_index("grp")
    x, c, y, z = grp // 2, lax.rem(grp, 2), blk // 4, lax.rem(blk, 4)
    yb = lax.rem(y, 2)
    tb = 1 - yb
    yp = y + 1 - 2 * yb
    yq = lax.rem(y + 3 + 2 * yb, 4)

    def device(x_, y_, z_, c_):
        return (y_ * 4 + z_, x_ * 2 + c_)

    me = device(x, y, z, c)
    sibling = device(x, y, z, 1 - c)
    img_peers = [
        (dx, dy, dc) for dy in range(2) for dx in range(4) for dc in range(2) if (dx, dy, dc) != (0, 0, 0)
    ]
    txt_peers = [(dz, dy) for dy in range(2) for dz in range(4) if (dz, dy) != (0, 0)]

    def img_peer(dx, dy, dc):
        return device(turn(x, dx), yp if dy else y, z, 1 - c if dc else c)

    def txt_peer(dz, dy):
        return device(x, yq if dy else y, turn(z, dz), c)

    own_copies = [
        pltpu.make_async_copy(src, dst, own_sem.at[i])
        for i, (src, dst) in enumerate(((img_in, embeds.at[0]), (txt_in, embeds.at[1]), (pairing_in, pairing_ref)))
    ]
    for copy in own_copies:
        copy.start()
    barrier = pltpu.get_barrier_semaphore()
    for p in img_peers:
        pl.semaphore_signal(barrier, inc=1, device_id=img_peer(*p), device_id_type=MESH)
    for p in txt_peers:
        pl.semaphore_signal(barrier, inc=1, device_id=txt_peer(*p), device_id_type=MESH)

    def pair_of(dx, dy):
        return flip(yb, dy) * 4 + turn(x, dx)

    def slot_of(dz, dy):
        return flip(tb, dy) * 4 + turn(z, dz)

    def img_region(dx, dy, low, rows, other=False):
        half = 1 - c if other else c
        return img.at[pair_of(dx, dy), pl.ds(pl.multiple_of(half * ROWS + low, 32), rows)]

    def txt_region(dz, dy, low, rows):
        return txt.at[slot_of(dz, dy), pl.ds(low, rows)]

    own_copies[0].wait()
    img_region(0, 0, 0, ROWS)[...] = normalize(embeds[0])[1].astype(bf16)
    own_copies[1].wait()
    txt_region(0, 0, 0, ROWS)[...] = normalize(embeds[1])[1].astype(bf16)

    msgs = Messages(send, recv)
    gat_i = Gather(msgs, img_region, img_peer(1, 0, 0), img_peer(3, 0, 0), img_peer(0, 1, 0), me)
    gat_t = Gather(msgs, txt_region, txt_peer(1, 0), txt_peer(3, 0), txt_peer(0, 1), me)
    both = (gat_i, gat_t)
    sib_k = msgs.take(9)

    def pieces(places):
        for place in places:
            if place == (2, 1):
                yield sib_k + 7, (*place, 0, 64)
                yield sib_k + 8, (*place, 64, 64)
            else:
                yield sib_k + ARRIVAL.index(place), (*place, 0, ROWS)

    def share(*places, only=(0, 1)):
        for i, (k, piece) in enumerate(pieces(places)):
            if i in only or len(places) > 1:
                ref = img_region(*piece)
                msgs.start(k, ref, ref, sibling)

    def shared(*places):
        for k, piece in pieces(places):
            msgs.arrived(k, img_region(*piece, other=True), me)

    pl.semaphore_wait(barrier, len(img_peers) + len(txt_peers))
    for g in both:
        g.go(10, 0, 5, 11, 1, 6)
    share((0, 0))

    scale = jnp.exp(jnp.full((1, 256), ls_ref[0], f32))
    factor = scale * (1.0 / CAP)
    for ref in (rowacc, colacc, rowk, colk, slacc, posacc):
        ref[...] = jnp.zeros_like(ref)

    def rows_of(slot):
        return pl.ds(pl.multiple_of(slot * ROWS, ROWS), ROWS)

    def forward(p, s):
        cos = lax.dot_general(txt[s], img_t[p], (((1,), (0,)), ((), ())), preferred_element_type=f32)
        bent = jnp.tanh(cos * factor)
        power = jnp.exp(CAP * bent)
        held = power * (1.0 - bent * bent)
        slope = held * cos
        cosr[p, rows_of(s)] = cos
        hr[p, rows_of(s)] = held
        colacc[s] += power[:, :ROWS] + power[:, ROWS:]
        colk[s] += slope[:, :ROWS] + slope[:, ROWS:]
        rowacc[p] += jnp.sum(power.reshape(16, 8, 256), axis=0)
        rowk[p] += jnp.sum(slope.reshape(16, 8, 256), axis=0)

    def pair_at(i):
        dx = jnp.where((i == 1) | (i == 5), 1, 0) + jnp.where((i == 2) | (i == 6), 3, 0)
        dx = dx + jnp.where((i == 4) | (i == 7), 2, 0)
        dy = jnp.where((i == 3) | (i >= 5), 1, 0)
        return flip(yb, dy) * 4 + turn(x, dx)

    slots = [slot_of(*place) for place in ARRIVAL]

    def batch(first, last, members, unroll=1):
        def body(i, carry):
            for j in members:
                forward(pair_at(i), slots[j])
            return carry

        lax.fori_loop(first, last, body, 0, unroll=unroll)

    def turned(*places):
        shared(*places)
        for place in places:
            p = pair_of(*place)
            img_t[p] = img[p].T

    turned((0, 0))
    batch(0, 1, (0,))
    for g in both:
        g.got(0, 5, 10)
        g.go(2, 7, 12, 3, 8, 15, 16)
    for g in both:
        g.got(1)
        g.go(13)
        g.got(6, 11)
    share((1, 0), (3, 0), (0, 1))
    batch(0, 1, (1, 2, 3))
    turned((1, 0), (3, 0), (0, 1))
    batch(1, 4, (0, 1, 2, 3))
    for g in both:
        g.got(7)
        g.go(14)
        g.got(2)
    share((2, 0))
    batch(0, 4, (4,), unroll=4)
    for g in both:
        g.got(3)
        g.go(4)
        g.got(8)
        g.go(9)
    turned((2, 0))
    batch(4, 5, (0, 1, 2, 3, 4))
    gat_i.got(12, 13, 15, 16)
    share((1, 1), (3, 1))
    gat_t.got(12, 13, 15, 16)
    batch(0, 5, (5, 6))
    turned((1, 1), (3, 1))
    batch(5, 6, (0, 1, 2, 3, 4, 5, 6))
    gat_i.got(4, 9)
    share((2, 1), only=(0,))
    batch(6, 7, (0, 1, 2, 3, 4, 5, 6))
    gat_i.got(14)
    share((2, 1), only=(1,))
    gat_t.got(4, 9, 14)
    batch(0, 7, (7,), unroll=7)
    turned((2, 1))
    batch(7, 8, (0, 1, 2, 3, 4, 5, 6, 7))

    img_me = yb * 8 + x * 2 + c
    txt_me = tb * 4 + z

    def img_index(dx, dy, dc):
        return flip(yb, dy) * 8 + turn(x, dx) * 2 + flip(c, dc)

    rows_all[img_me] = jnp.concatenate([jnp.sum(rowacc[p], axis=0, keepdims=True) for p in range(8)], axis=0)
    k_rows = msgs.take(len(img_peers))
    for i, p in enumerate(img_peers):
        msgs.start(k_rows + i, rows_all.at[img_me], rows_all.at[img_me], img_peer(*p))
    cols_all[txt_me] = jnp.concatenate(
        [jnp.sum(colacc[s].T, axis=0, keepdims=True) for s in range(8)], axis=0
    )
    k_cols = msgs.take(len(txt_peers))
    for i, p in enumerate(txt_peers):
        msgs.start(k_cols + i, cols_all.at[txt_me], cols_all.at[txt_me], txt_peer(*p))

    def collect_img(first, ref):
        for i, (dx, dy, dc) in enumerate(img_peers):
            msgs.arrived(first + i, ref.at[img_index((4 - dx) % 4, dy, dc)], me)

    def collect_txt(first, ref):
        for i, (dz, dy) in enumerate(txt_peers):
            msgs.arrived(first + i, ref.at[slot_of((4 - dz) % 4, dy)], me)

    def add_up(ref, first, last):
        total = ref[first]
        for i in range(first + 1, last):
            total = total + ref[i]
        return total

    own_copies[2].wait()
    lane = lax.broadcasted_iota(jnp.int32, (ROWS, 256), 1)
    diagonal = lane == lax.broadcasted_iota(jnp.int32, (ROWS, 256), 0) + c * ROWS
    pair_mine = (pair_of(0, 0), pair_of(0, 1))

    def matching(s, carry):
        slot_blk = jnp.where(s // 4 == tb, y, yq) * 4 + lax.rem(s, 4)
        for dy in range(2):
            partner_of = pairing_ref[(yp if dy else y) * 4 + z]
            match = jnp.where(partner_of == slot_blk, 1.0, 0.0).astype(f32)
            partner = jnp.where(diagonal, match, 0.0)
            cos = cosr[pair_mine[dy], rows_of(s)]
            bent = jnp.tanh(cos * factor)
            taken = scale * (partner * (1.0 - bent * bent))
            diag[dy, rows_of(s)] = taken
            posacc[...] += jnp.sum((CAP * bent * partner).reshape(16, 8, 256), axis=0)
            slacc[...] += jnp.sum((taken * cos).reshape(16, 8, 256), axis=0)
        return carry

    lax.fori_loop(0, 8, matching, 0, unroll=2)
    row_slope = jnp.concatenate([jnp.sum(rowk[p], axis=0, keepdims=True) for p in range(8)], axis=0)
    col_slope = jnp.concatenate([jnp.sum(colk[s].T, axis=0, keepdims=True) for s in range(8)], axis=0)
    for g in both:
        g.sent(*range(17))
    msgs.sent(*range(sib_k, sib_k + 9))

    collect_txt(k_cols, cols_all)
    col_sum = add_up(cols_all, 0, 8)
    col_weight = (0.5 * scale[:, :ROWS]) / col_sum
    for s in range(8):
        bmat[s] = jnp.broadcast_to(col_weight[s : s + 1], (ROWS, ROWS)).T
    collect_img(k_rows, rows_all)
    row_sum = add_up(rows_all, 0, 16)
    row_weight = (0.5 * scale) / row_sum
    for p in range(8):
        arow[p] = row_weight[p : p + 1]

    def tile(p, s, matched=None):
        b = bmat[s]
        g = hr[p, rows_of(s)] * (arow[p] + jnp.concatenate([b, b], axis=1))
        if matched is not None:
            g = g - diag[matched, rows_of(s)]
        gr[p, rows_of(s)] = g.astype(bf16)

    def gradient(place, first=1):
        p = pair_of(*place)

        def body(i, carry):
            tile(p, lax.rem(slot_of(2, 1) + i, 8), place[1] if place[0] == 0 else None)
            return carry

        lax.fori_loop(first, 8, body, 0, unroll=4 if first == 0 else 7)

    def send_sums():
        sub = lax.broadcasted_iota(jnp.int32, (8, 256), 0)
        half = lax.broadcasted_iota(jnp.int32, (8, 256), 1) // ROWS
        row_part = jnp.where((sub == pair_mine[0]) & (half == c), jnp.log(row_sum), 0.0) - 2.0 * posacc[...]
        col_part = jnp.where(sub[:, :ROWS] == txt_me, jnp.log(col_sum), 0.0)
        slope = row_weight * row_slope - slacc[...]
        sc_all[img_me, pl.ds(0, 8)] = row_part[:, :ROWS] + row_part[:, ROWS:] + col_part
        sc_all[img_me, pl.ds(8, 8)] = slope[:, :ROWS] + slope[:, ROWS:] + col_weight * col_slope
        for i, p in enumerate(img_peers):
            msgs.start(k_sc + i, sc_all.at[img_me], sc_all.at[img_me], img_peer(*p))

    k_sc = msgs.take(len(img_peers))

    k_sib = msgs.take(8)
    own = pl.ds(pl.multiple_of(c * ROWS, ROWS), ROWS)
    others = pl.ds(pl.multiple_of((1 - c) * ROWS, ROWS), ROWS)

    def img_part(place, low, rows):
        return gi.at[REDUCE.index(place), pl.ds(pl.multiple_of(c * ROWS + low, 32), rows)]

    def txt_part(place, low, rows):
        return gt.at[REDUCE.index(place), pl.ds(low, rows)]

    red_i = Reduce(msgs, img_part, land_i, img_peer(1, 0, 0), img_peer(3, 0, 0), img_peer(0, 1, 0), me)
    red_t = Reduce(msgs, txt_part, land_t, txt_peer(1, 0), txt_peer(3, 0), txt_peer(0, 1), me)
    k_mid = msgs.take(len(txt_peers))

    def img_product(i):
        gi[i] = lax.dot_general(
            gr[pair_of(*REDUCE[i])], txt[...].reshape(8 * ROWS, D), (((0,), (0,)), ((), ())), preferred_element_type=f32
        ).astype(bf16)
        msgs.start(k_sib + i, gi.at[i, others], gi_sib.at[i], sibling)

    def img_send(i):
        msgs.arrived(k_sib + i, gi_sib.at[i], me)
        gi[i, own] = (gi[i, own].astype(f32) + gi_sib[i].astype(f32)).astype(bf16)
        red_i.step(i)

    def txt_product(i):
        s = slot_of(*REDUCE[i])
        lhs = jnp.concatenate([gr[q, rows_of(s)] for q in range(8)], axis=1)
        gt[i] = lax.dot_general(
            lhs, img[...].reshape(16 * ROWS, D), (((1,), (0,)), ((), ())), preferred_element_type=f32
        ).astype(bf16)
        red_t.step(i)

    gradient(REDUCE[0], 0)
    for place in REDUCE[1:]:
        tile(pair_of(*place), slot_of(2, 1), place[1] if place[0] == 0 else None)
    img_product(0)
    txt_product(0)
    for place in REDUCE[1:]:
        gradient(place)
    img_send(0)
    send_sums()
    for i in range(1, 8):
        img_product(i)
        if i > 1:
            img_send(i - 1)
        txt_product(i)
        if i == 3:
            collect_img(k_sc, sc_all)
            sc_mid[txt_me] = add_up(sc_all, 0, 16)
            for j, peer in enumerate(txt_peers):
                msgs.start(k_mid + j, sc_mid.at[txt_me], sc_mid.at[txt_me], txt_peer(*peer))
    img_send(7)
    for r in (red_i, red_t):
        r.last()
    for r in (red_i, red_t):
        r.last_ring()
    collect_txt(k_mid, sc_mid)
    sums[...] = add_up(sc_mid, 0, 4) + add_up(sc_mid, 4, 8)
    out_copies = [pltpu.make_async_copy(sums, sums_out, own_sem.at[3])]
    out_copies[0].start()
    for first, count in ((k_rows, 15), (k_cols, 7), (k_sc, 15), (k_mid, 7), (k_sib, 8)):
        msgs.sent(*range(first, first + count))
    for r in (red_i, red_t):
        r.sent(*range(12))
    for low, ks in ((64, (7, 14, 16)), (0, (13, 15, 12))):
        for n, (r, out) in enumerate(((red_i, gi_out), (red_t, gt_out))):
            part = pl.ds(low, 64)
            units[n, part] = r.total(low, *ks)
            copy = pltpu.make_async_copy(units.at[n, part], out.at[part], own_sem.at[3 + len(out_copies)])
            copy.start()
            out_copies.append(copy)
    msgs.finish()
    for copy in out_copies:
        copy.wait()


def epilogue(sums_in, img_in, txt_in, gi_in, gt_in, gi_out, gt_out, loss_out, gls_out, sums, embeds, units, sem):
    sums_copy = pltpu.make_async_copy(sums_in, sums, sem.at[0])
    ins, outs = [], []
    for low in (0, 64):
        for n, (embed, unit, out) in enumerate(((img_in, gi_in, gi_out), (txt_in, gt_in, gt_out))):
            k = 1 + 3 * len(ins)
            part = pl.ds(low, 64)
            ins.append((
                pltpu.make_async_copy(embed.at[part], embeds.at[n, part], sem.at[k]),
                pltpu.make_async_copy(unit.at[part], units.at[n, part], sem.at[k + 1]),
            ))
            outs.append((n, part, pltpu.make_async_copy(units.at[n, part], out.at[part], sem.at[k + 2])))
    for pair in ins:
        for copy in pair:
            copy.start()
    sums_copy.start()
    for pair, (n, part, out) in zip(ins, outs):
        for copy in pair:
            copy.wait()
        inverse, unit = normalize(embeds[n, part])
        grad_unit = units[n, part]
        inner = jnp.sum(unit * grad_unit, axis=1, keepdims=True)
        units[n, part] = inverse * (grad_unit - unit * inner)
        out.start()
    sums_copy.wait()
    loss_out[0] = jnp.sum(sums[:8]) * (1.0 / (2.0 * BATCH))
    gls_out[0] = jnp.sum(sums[8:]) * (1.0 / BATCH)
    for _, _, out in outs:
        out.wait()


N_MSG = 17 + 17 + 9 + 15 + 7 + 15 + 8 + 17 + 17 + 7


def local(image_embed, text_embed, log_scale, pairing):
    vmem, smem = pltpu.VMEM, pltpu.SMEM
    anywhere, in_smem = pl.BlockSpec(memory_space=pl.ANY), pl.BlockSpec(memory_space=smem)
    grad = jax.ShapeDtypeStruct((ROWS, D), f32)
    scalar = jax.ShapeDtypeStruct((1,), f32)
    unit_img, unit_txt, sums = pl.pallas_call(
        kernel,
        out_shape=[grad, grad, jax.ShapeDtypeStruct((16, ROWS), f32)],
        in_specs=[in_smem] + [anywhere] * 3,
        out_specs=[anywhere] * 3,
        scratch_shapes=[
            vmem((8, 256, D), bf16),
            vmem((8, D, 256), bf16),
            vmem((8, ROWS, D), bf16),
            vmem((8, 1024, 256), f32),
            vmem((8, 1024, 256), f32),
            vmem((8, 1024, 256), bf16),
            vmem((8, 8, 256), f32),
            vmem((8, ROWS, ROWS), f32),
            vmem((8, 8, 256), f32),
            vmem((8, ROWS, ROWS), f32),
            vmem((8, 1, 256), f32),
            vmem((8, ROWS, ROWS), f32),
            vmem((2, 1024, 256), f32),
            vmem((8, 256), f32),
            vmem((8, 256), f32),
            vmem((16, 8, 256), f32),
            vmem((8, 8, ROWS), f32),
            vmem((16, 16, ROWS), f32),
            vmem((8, 16, ROWS), f32),
            vmem((8, 256, D), bf16),
            vmem((8, ROWS, D), bf16),
            vmem((8, ROWS, D), bf16),
            vmem((LAND, D), bf16),
            vmem((LAND, D), bf16),
            smem((16,), jnp.int32),
            vmem((2, ROWS, D), bf16),
            vmem((2, ROWS, D), f32),
            vmem((16, ROWS), f32),
            pltpu.SemaphoreType.DMA((8,)),
            pltpu.SemaphoreType.DMA((N_MSG,)),
            pltpu.SemaphoreType.DMA((N_MSG,)),
        ],
        compiler_params=pltpu.CompilerParams(
            collective_id=0, has_side_effects=True, vmem_limit_bytes=60 * 1024 * 1024
        ),
        name="contrast",
    )(log_scale, pairing, image_embed, text_embed)
    return pl.pallas_call(
        epilogue,
        out_shape=[grad, grad, scalar, scalar],
        in_specs=[anywhere] * 5,
        out_specs=[anywhere] * 2 + [in_smem] * 2,
        scratch_shapes=[
            vmem((16, ROWS), f32),
            vmem((2, ROWS, D), bf16),
            vmem((2, ROWS, D), f32),
            pltpu.SemaphoreType.DMA((13,)),
        ],
        compiler_params=pltpu.CompilerParams(vmem_limit_bytes=60 * 1024 * 1024),
        name="back_norm",
    )(sums, image_embed, text_embed, unit_img, unit_txt)


def solution(mesh):
    return jax.shard_map(
        local,
        mesh=mesh,
        in_specs=(P(("blk", "grp"), None), P(("blk", "grp"), None), P(), P()),
        out_specs=(P(("blk", "grp"), None), P(("blk", "grp"), None), P(), P()),
        check_vma=False,
    )
```

```python
import jax
import jax.numpy as jnp
from jax import lax
from jax.experimental import pallas as pl
from jax.experimental.pallas import tpu as pltpu
from jax.sharding import PartitionSpec as P

f32, bf16 = jnp.float32, jnp.bfloat16
MESH = pl.DeviceIdType.MESH
CAP = 30.0
ROWS, D, BATCH = 128, 1280, 16384
ARRIVAL = ((0, 0), (1, 0), (3, 0), (0, 1), (2, 0), (1, 1), (3, 1), (2, 1))
REDUCE = ((2, 1), (2, 0), (1, 1), (3, 1), (0, 1), (1, 0), (3, 0), (0, 0))
LAND_AT = (0, 32, 64, 128, 192, 256, 320, 384, 448, 480, 512, 544, 576, 640, 704, 768, 832)
LAND_ROWS = (32, 32, 64, 64, 64, 64, 64, 64, 32, 32, 32, 32, 64, 64, 64, 64, 64)
LAND = 896


def flip(bit, by):
    return bit + by - 2 * bit * by


def turn(place, by):
    return lax.rem(place + by, 4)


class Messages:
    def __init__(self, send, recv):
        self.send, self.recv, self.count, self.open = send, recv, 0, {}

    def take(self, count):
        first = self.count
        self.count += count
        return first

    def start(self, k, src, dst, device):
        copy = pltpu.make_async_remote_copy(
            src, dst, self.send.at[k], self.recv.at[k], device_id=device, device_id_type=MESH
        )
        copy.start()
        self.open[k] = copy

    def arrived(self, k, region, device):
        pltpu.make_async_remote_copy(
            region, region, self.send.at[k], self.recv.at[k], device_id=device, device_id_type=MESH
        ).wait_recv()

    def sent(self, *ks):
        for k in ks:
            self.open.pop(k).wait_send()

    def finish(self):
        self.sent(*list(self.open))


class Gather:
    def __init__(self, msgs, region, plus, minus, pair, me, relay=None):
        self.m, self.region, self.me, self.relay = msgs, region, me, relay
        self.plus, self.minus, self.pair = plus, minus, pair
        self.k = msgs.take(17)

    TABLE = (
        ("plus", (0, 0, 0, 64), (3, 0, 0, 64)),
        ("plus", (0, 0, 64, 64), (3, 0, 64, 64)),
        ("plus", (3, 0, 0, 64), (2, 0, 0, 64)),
        ("plus", (0, 1, 0, 32), (3, 1, 0, 32)),
        ("plus", (3, 1, 0, 32), (2, 1, 0, 32)),
        ("minus", (0, 0, 64, 64), (1, 0, 64, 64)),
        ("minus", (0, 0, 0, 64), (1, 0, 0, 64)),
        ("minus", (1, 0, 64, 64), (2, 0, 64, 64)),
        ("minus", (0, 1, 32, 32), (1, 1, 32, 32)),
        ("minus", (1, 1, 32, 32), (2, 1, 32, 32)),
        ("pair", (0, 0, 0, 64), (0, 1, 0, 64)),
        ("pair", (0, 0, 64, 64), (0, 1, 64, 64)),
        ("pair", (1, 0, 64, 64), (1, 1, 64, 64)),
        ("pair", (3, 0, 64, 64), (3, 1, 64, 64)),
        ("pair", (2, 0, 64, 64), (2, 1, 64, 64)),
        ("plus", (0, 1, 32, 32), (3, 1, 32, 32)),
        ("minus", (0, 1, 0, 32), (1, 1, 0, 32)),
    )

    def go(self, *ks):
        for k in ks:
            way, here, _ = self.TABLE[k]
            ref = self.region(*here)
            self.m.start(self.k + k, ref, ref, getattr(self, way))

    def sent(self, *ks):
        self.m.sent(*(self.k + k for k in ks))

    def got(self, *ks):
        for k in ks:
            self.m.arrived(self.k + k, self.region(*self.TABLE[k][2]), self.me)
            if self.relay is not None:
                self.relay(k, self.TABLE[k][2])


class Reduce:
    TABLE = (
        ("plus", (2, 1), 0, 32),
        ("minus", (2, 1), 32, 32),
        ("pair", (2, 1), 64, 64),
        ("pair", (1, 1), 64, 64),
        ("plus", (1, 1), 0, 64),
        ("pair", (3, 1), 64, 64),
        ("minus", (3, 1), 0, 64),
        ("pair", (0, 1), 64, 64),
        ("plus", (2, 0), 0, 32),
        ("minus", (2, 0), 32, 32),
        ("plus", (2, 0), 64, 32),
        ("minus", (2, 0), 96, 32),
        ("pair", (0, 1), 0, 64),
        ("plus", (1, 0), 0, 64),
        ("plus", (1, 0), 64, 64),
        ("minus", (3, 0), 0, 64),
        ("minus", (3, 0), 64, 64),
    )

    def __init__(self, msgs, part, land, plus, minus, pair, me):
        self.m, self.part, self.land, self.me = msgs, part, land, me
        self.plus, self.minus, self.pair = plus, minus, pair
        self.k = msgs.take(17)

    def where(self, k):
        return self.land.at[pl.ds(LAND_AT[k], LAND_ROWS[k])]

    def go(self, *ks):
        for k in ks:
            way, place, low, rows = self.TABLE[k]
            self.m.start(self.k + k, self.part(place, low, rows), self.where(k), getattr(self, way))

    def sent(self, *ks):
        self.m.sent(*(self.k + k for k in ks))

    def got(self, *ks):
        for k in ks:
            self.m.arrived(self.k + k, self.where(k), self.me)

    def add(self, place, low, rows, *landed):
        ref = self.part(place, low, rows)
        total = ref[...].astype(f32)
        for at in landed:
            total = total + self.land[pl.ds(at, rows)].astype(f32)
        ref[...] = total.astype(bf16)

    def step(self, i):
        if i == 0:
            self.go(0, 1, 2)
        if i == 1:
            self.go(8, 9)
        if i == 2:
            self.go(3)
            self.got(0)
            self.add((1, 1), 0, 32, LAND_AT[0])
            self.go(4)
        if i == 3:
            self.go(5)
            self.got(1)
            self.add((3, 1), 32, 32, LAND_AT[1])
            self.go(6)
        if i == 4:
            self.go(7)
            self.got(2)
            self.add((2, 0), 64, 64, LAND_AT[2])
            self.go(10, 11)
        if i == 5:
            self.got(8)
            self.add((1, 0), 0, 32, LAND_AT[8])
            self.go(13)
        if i == 6:
            self.got(9)
            self.add((3, 0), 32, 32, LAND_AT[9])
            self.go(15)

    def last(self):
        self.got(4, 6)
        self.add((0, 1), 0, 64, LAND_AT[4], LAND_AT[6])
        self.go(12)
        self.got(3)
        self.add((1, 0), 64, 64, LAND_AT[3])
        self.got(10)
        self.add((1, 0), 64, 32, LAND_AT[10])
        self.go(14)

    def last_ring(self):
        self.got(5)
        self.add((3, 0), 64, 64, LAND_AT[5])
        self.got(11)
        self.add((3, 0), 96, 32, LAND_AT[11])
        self.go(16)

    def total(self, low, *ks):
        self.got(*ks)
        total = self.part((0, 0), low, 64)[...].astype(f32)
        for k in ks:
            total = total + self.where(k)[...].astype(f32)
        return total


def normalize(embed):
    wide = embed.astype(f32)
    inverse = lax.rsqrt(jnp.sum(wide * wide, axis=1, keepdims=True) + 1e-06)
    return inverse, wide * inverse


def kernel(
    ls_ref, pairing_in, img_in, txt_in,
    gi_out, gt_out, sums_out,
    img, img_t, txt, cosr, hr, gr, rowacc, colacc, rowk, colk, arow, bmat, diag, slacc, posacc,
    rows_all, cols_all, sc_all, sc_mid,
    gi, gi_sib, gt, land_i, land_t,
    pairing_ref, embeds, units, sums, own_sem, send, recv,
):
    blk, grp = lax.axis_index("blk"), lax.axis_index("grp")
    x, c, y, z = grp // 2, lax.rem(grp, 2), blk // 4, lax.rem(blk, 4)
    yb = lax.rem(y, 2)
    tb = 1 - yb
    yp = y + 1 - 2 * yb
    yq = lax.rem(y + 3 + 2 * yb, 4)

    def device(x_, y_, z_, c_):
        return (y_ * 4 + z_, x_ * 2 + c_)

    me = device(x, y, z, c)
    sibling = device(x, y, z, 1 - c)
    img_peers = [
        (dx, dy, dc) for dy in range(2) for dx in range(4) for dc in range(2) if (dx, dy, dc) != (0, 0, 0)
    ]
    txt_peers = [(dz, dy) for dy in range(2) for dz in range(4) if (dz, dy) != (0, 0)]

    def img_peer(dx, dy, dc):
        return device(turn(x, dx), yp if dy else y, z, 1 - c if dc else c)

    def txt_peer(dz, dy):
        return device(x, yq if dy else y, turn(z, dz), c)

    own_copies = [
        pltpu.make_async_copy(src, dst, own_sem.at[i])
        for i, (src, dst) in enumerate(((img_in, embeds.at[0]), (txt_in, embeds.at[1]), (pairing_in, pairing_ref)))
    ]
    for copy in own_copies:
        copy.start()
    barrier = pltpu.get_barrier_semaphore()
    for p in img_peers:
        pl.semaphore_signal(barrier, inc=1, device_id=img_peer(*p), device_id_type=MESH)
    for p in txt_peers:
        pl.semaphore_signal(barrier, inc=1, device_id=txt_peer(*p), device_id_type=MESH)

    def pair_of(dx, dy):
        return flip(yb, dy) * 4 + turn(x, dx)

    def slot_of(dz, dy):
        return flip(tb, dy) * 4 + turn(z, dz)

    def img_region(dx, dy, low, rows, other=False):
        half = 1 - c if other else c
        return img.at[pair_of(dx, dy), pl.ds(pl.multiple_of(half * ROWS + low, 32), rows)]

    def txt_region(dz, dy, low, rows):
        return txt.at[slot_of(dz, dy), pl.ds(low, rows)]

    own_copies[0].wait()
    img_region(0, 0, 0, ROWS)[...] = normalize(embeds[0])[1].astype(bf16)
    own_copies[1].wait()
    txt_region(0, 0, 0, ROWS)[...] = normalize(embeds[1])[1].astype(bf16)

    msgs = Messages(send, recv)
    sib_k = msgs.take(18)

    def share(k, region):
        ref = img_region(*region)
        msgs.start(sib_k + k, ref, ref, sibling)

    gat_i = Gather(msgs, img_region, img_peer(1, 0, 0), img_peer(3, 0, 0), img_peer(0, 1, 0), me, share)
    gat_t = Gather(msgs, txt_region, txt_peer(1, 0), txt_peer(3, 0), txt_peer(0, 1), me)
    both = (gat_i, gat_t)

    def shared(place):
        pieces = [(k, entry[2]) for k, entry in enumerate(Gather.TABLE) if entry[2][:2] == place]
        for k, region in pieces or [(17, (0, 0, 0, ROWS))]:
            msgs.arrived(sib_k + k, img_region(*region, other=True), me)

    pl.semaphore_wait(barrier, len(img_peers) + len(txt_peers))
    for g in both:
        g.go(10, 0, 5, 11, 1, 6)
    share(17, (0, 0, 0, ROWS))

    scale = jnp.exp(jnp.full((1, 256), ls_ref[0], f32))
    factor = scale * (1.0 / CAP)
    for ref in (rowacc, colacc, rowk, colk, slacc, posacc):
        ref[...] = jnp.zeros_like(ref)

    def rows_of(slot):
        return pl.ds(pl.multiple_of(slot * ROWS, ROWS), ROWS)

    def forward(p, s):
        cos = lax.dot_general(txt[s], img_t[p], (((1,), (0,)), ((), ())), preferred_element_type=f32)
        bent = jnp.tanh(cos * factor)
        power = jnp.exp(CAP * bent)
        held = power * (1.0 - bent * bent)
        slope = held * cos
        cosr[p, rows_of(s)] = cos
        hr[p, rows_of(s)] = held
        colacc[s] += power[:, :ROWS] + power[:, ROWS:]
        colk[s] += slope[:, :ROWS] + slope[:, ROWS:]
        rowacc[p] += jnp.sum(power.reshape(16, 8, 256), axis=0)
        rowk[p] += jnp.sum(slope.reshape(16, 8, 256), axis=0)

    def pair_at(i):
        dx = jnp.where((i == 1) | (i == 5), 1, 0) + jnp.where((i == 2) | (i == 6), 3, 0)
        dx = dx + jnp.where((i == 4) | (i == 7), 2, 0)
        dy = jnp.where((i == 3) | (i >= 5), 1, 0)
        return flip(yb, dy) * 4 + turn(x, dx)

    slots = [slot_of(*place) for place in ARRIVAL]

    def batch(first, last, members, unroll=1):
        def body(i, carry):
            for j in members:
                forward(pair_at(i), slots[j])
            return carry

        lax.fori_loop(first, last, body, 0, unroll=unroll)

    def turned(place):
        shared(place)
        p = pair_of(*place)
        img_t[p] = img[p].T

    turned((0, 0))
    batch(0, 1, (0,))
    for g in both:
        g.got(0, 5, 10)
        g.go(2, 7, 12, 3, 8, 15, 16)
    for g in both:
        g.got(1)
        g.go(13)
        g.got(6, 11)
    batch(0, 1, (1, 2, 3))
    turned((1, 0))
    batch(1, 2, (0, 1, 2, 3))
    turned((3, 0))
    batch(2, 3, (0, 1, 2, 3))
    for g in both:
        g.got(7)
        g.go(14)
        g.got(2, 12)
    turned((0, 1))
    batch(3, 4, (0, 1, 2, 3))
    batch(0, 4, (4,), unroll=4)
    turned((2, 0))
    for g in both:
        g.got(3)
        g.go(4)
        g.got(8)
        g.go(9)
    batch(4, 5, (0, 1, 2, 3, 4))
    for g in both:
        g.got(13, 15, 16)
    batch(0, 5, (5, 6), unroll=5)
    turned((1, 1))
    batch(5, 6, (0, 1, 2, 3, 4, 5, 6))
    gat_i.got(4, 9)
    turned((3, 1))
    batch(6, 7, (0, 1, 2, 3, 4, 5, 6))
    gat_i.got(14)
    gat_t.got(4, 9, 14)
    batch(0, 7, (7,), unroll=7)
    turned((2, 1))
    batch(7, 8, (0, 1, 2, 3, 4, 5, 6, 7))

    img_me = yb * 8 + x * 2 + c
    txt_me = tb * 4 + z

    def img_index(dx, dy, dc):
        return flip(yb, dy) * 8 + turn(x, dx) * 2 + flip(c, dc)

    rows_all[img_me] = jnp.concatenate([jnp.sum(rowacc[p], axis=0, keepdims=True) for p in range(8)], axis=0)
    k_rows = msgs.take(len(img_peers))
    for i, p in enumerate(img_peers):
        msgs.start(k_rows + i, rows_all.at[img_me], rows_all.at[img_me], img_peer(*p))
    cols_all[txt_me] = jnp.concatenate(
        [jnp.sum(colacc[s].T, axis=0, keepdims=True) for s in range(8)], axis=0
    )
    k_cols = msgs.take(len(txt_peers))
    for i, p in enumerate(txt_peers):
        msgs.start(k_cols + i, cols_all.at[txt_me], cols_all.at[txt_me], txt_peer(*p))

    def collect_img(first, ref):
        for i, (dx, dy, dc) in enumerate(img_peers):
            msgs.arrived(first + i, ref.at[img_index((4 - dx) % 4, dy, dc)], me)

    def collect_txt(first, ref):
        for i, (dz, dy) in enumerate(txt_peers):
            msgs.arrived(first + i, ref.at[slot_of((4 - dz) % 4, dy)], me)

    def add_up(ref, first, last):
        total = ref[first]
        for i in range(first + 1, last):
            total = total + ref[i]
        return total

    own_copies[2].wait()
    lane = lax.broadcasted_iota(jnp.int32, (ROWS, 256), 1)
    diagonal = lane == lax.broadcasted_iota(jnp.int32, (ROWS, 256), 0) + c * ROWS
    pair_mine = (pair_of(0, 0), pair_of(0, 1))

    def matching(s, carry):
        slot_blk = jnp.where(s // 4 == tb, y, yq) * 4 + lax.rem(s, 4)
        for dy in range(2):
            partner_of = pairing_ref[(yp if dy else y) * 4 + z]
            match = jnp.where(partner_of == slot_blk, 1.0, 0.0).astype(f32)
            partner = jnp.where(diagonal, match, 0.0)
            cos = cosr[pair_mine[dy], rows_of(s)]
            bent = jnp.tanh(cos * factor)
            taken = scale * (partner * (1.0 - bent * bent))
            diag[dy, rows_of(s)] = taken
            posacc[...] += jnp.sum((CAP * bent * partner).reshape(16, 8, 256), axis=0)
            slacc[...] += jnp.sum((taken * cos).reshape(16, 8, 256), axis=0)
        return carry

    lax.fori_loop(0, 8, matching, 0, unroll=2)
    row_slope = jnp.concatenate([jnp.sum(rowk[p], axis=0, keepdims=True) for p in range(8)], axis=0)
    col_slope = jnp.concatenate([jnp.sum(colk[s].T, axis=0, keepdims=True) for s in range(8)], axis=0)
    for g in both:
        g.sent(*range(17))
    msgs.sent(*range(sib_k, sib_k + 18))

    collect_txt(k_cols, cols_all)
    col_sum = add_up(cols_all, 0, 8)
    col_weight = (0.5 * scale[:, :ROWS]) / col_sum
    for s in range(8):
        bmat[s] = jnp.broadcast_to(col_weight[s : s + 1], (ROWS, ROWS)).T
    collect_img(k_rows, rows_all)
    row_sum = add_up(rows_all, 0, 16)
    row_weight = (0.5 * scale) / row_sum
    for p in range(8):
        arow[p] = row_weight[p : p + 1]

    def tile(p, s, matched=None):
        b = bmat[s]
        g = hr[p, rows_of(s)] * (arow[p] + jnp.concatenate([b, b], axis=1))
        if matched is not None:
            g = g - diag[matched, rows_of(s)]
        gr[p, rows_of(s)] = g.astype(bf16)

    def gradient(place, first=1):
        p = pair_of(*place)

        def body(i, carry):
            tile(p, lax.rem(slot_of(2, 1) + i, 8), place[1] if place[0] == 0 else None)
            return carry

        lax.fori_loop(first, 8, body, 0, unroll=4 if first == 0 else 7)

    def send_sums():
        sub = lax.broadcasted_iota(jnp.int32, (8, 256), 0)
        half = lax.broadcasted_iota(jnp.int32, (8, 256), 1) // ROWS
        row_part = jnp.where((sub == pair_mine[0]) & (half == c), jnp.log(row_sum), 0.0) - 2.0 * posacc[...]
        col_part = jnp.where(sub[:, :ROWS] == txt_me, jnp.log(col_sum), 0.0)
        slope = row_weight * row_slope - slacc[...]
        sc_all[img_me, pl.ds(0, 8)] = row_part[:, :ROWS] + row_part[:, ROWS:] + col_part
        sc_all[img_me, pl.ds(8, 8)] = slope[:, :ROWS] + slope[:, ROWS:] + col_weight * col_slope
        for i, p in enumerate(img_peers):
            msgs.start(k_sc + i, sc_all.at[img_me], sc_all.at[img_me], img_peer(*p))

    k_sc = msgs.take(len(img_peers))

    k_sib = msgs.take(8)
    own = pl.ds(pl.multiple_of(c * ROWS, ROWS), ROWS)
    others = pl.ds(pl.multiple_of((1 - c) * ROWS, ROWS), ROWS)

    def img_part(place, low, rows):
        return gi.at[REDUCE.index(place), pl.ds(pl.multiple_of(c * ROWS + low, 32), rows)]

    def txt_part(place, low, rows):
        return gt.at[REDUCE.index(place), pl.ds(low, rows)]

    red_i = Reduce(msgs, img_part, land_i, img_peer(1, 0, 0), img_peer(3, 0, 0), img_peer(0, 1, 0), me)
    red_t = Reduce(msgs, txt_part, land_t, txt_peer(1, 0), txt_peer(3, 0), txt_peer(0, 1), me)
    k_mid = msgs.take(len(txt_peers))

    def img_product(i):
        gi[i] = lax.dot_general(
            gr[pair_of(*REDUCE[i])], txt[...].reshape(8 * ROWS, D), (((0,), (0,)), ((), ())), preferred_element_type=f32
        ).astype(bf16)
        msgs.start(k_sib + i, gi.at[i, others], gi_sib.at[i], sibling)

    def img_send(i):
        msgs.arrived(k_sib + i, gi_sib.at[i], me)
        gi[i, own] = (gi[i, own].astype(f32) + gi_sib[i].astype(f32)).astype(bf16)
        red_i.step(i)

    def txt_product(i):
        s = slot_of(*REDUCE[i])
        lhs = jnp.concatenate([gr[q, rows_of(s)] for q in range(8)], axis=1)
        gt[i] = lax.dot_general(
            lhs, img[...].reshape(16 * ROWS, D), (((1,), (0,)), ((), ())), preferred_element_type=f32
        ).astype(bf16)
        red_t.step(i)

    gradient(REDUCE[0], 0)
    for place in REDUCE[1:]:
        tile(pair_of(*place), slot_of(2, 1), place[1] if place[0] == 0 else None)
    img_product(0)
    txt_product(0)
    for place in REDUCE[1:]:
        gradient(place)
    img_send(0)
    for i in range(1, 8):
        img_product(i)
        if i > 1:
            img_send(i - 1)
        txt_product(i)
        if i == 1:
            send_sums()
        if i == 4:
            collect_img(k_sc, sc_all)
            sc_mid[txt_me] = add_up(sc_all, 0, 16)
            for j, peer in enumerate(txt_peers):
                msgs.start(k_mid + j, sc_mid.at[txt_me], sc_mid.at[txt_me], txt_peer(*peer))
    img_send(7)
    for r in (red_i, red_t):
        r.last()
    for r in (red_i, red_t):
        r.last_ring()
    collect_txt(k_mid, sc_mid)
    sums[...] = add_up(sc_mid, 0, 4) + add_up(sc_mid, 4, 8)
    out_copies = [pltpu.make_async_copy(sums, sums_out, own_sem.at[3])]
    out_copies[0].start()
    for first, count in ((k_rows, 15), (k_cols, 7), (k_sc, 15), (k_mid, 7), (k_sib, 8)):
        msgs.sent(*range(first, first + count))
    for r in (red_i, red_t):
        r.sent(*range(12))
    for low, ks in ((64, (7, 14, 16)), (0, (13, 15, 12))):
        for n, (r, out) in enumerate(((red_i, gi_out), (red_t, gt_out))):
            part = pl.ds(low, 64)
            units[n, part] = r.total(low, *ks)
            copy = pltpu.make_async_copy(units.at[n, part], out.at[part], own_sem.at[3 + len(out_copies)])
            copy.start()
            out_copies.append(copy)
    msgs.finish()
    for copy in out_copies:
        copy.wait()


def epilogue(sums, img_in, txt_in, gi_in, gt_in, gi_out, gt_out, loss_out, gls_out):
    for embed, grad, out in ((img_in, gi_in, gi_out), (txt_in, gt_in, gt_out)):
        inverse, unit = normalize(embed[...])
        grad_unit = grad[...]
        inner = jnp.sum(unit * grad_unit, axis=1, keepdims=True)
        out[...] = inverse * (grad_unit - unit * inner)
    loss_out[0] = jnp.sum(sums[:8]) * (1.0 / (2.0 * BATCH))
    gls_out[0] = jnp.sum(sums[8:]) * (1.0 / BATCH)


N_MSG = 17 + 17 + 18 + 15 + 7 + 15 + 8 + 17 + 17 + 7


def local(image_embed, text_embed, log_scale, pairing):
    vmem, smem = pltpu.VMEM, pltpu.SMEM
    in_hbm, in_vmem, in_smem = (pl.BlockSpec(memory_space=m) for m in (pltpu.HBM, vmem, smem))
    grad = jax.ShapeDtypeStruct((ROWS, D), f32)
    scalar = jax.ShapeDtypeStruct((1,), f32)
    unit_img, unit_txt, sums = pl.pallas_call(
        kernel,
        out_shape=[grad, grad, jax.ShapeDtypeStruct((16, ROWS), f32)],
        in_specs=[in_smem] + [in_hbm] * 3,
        out_specs=[in_hbm] * 3,
        scratch_shapes=[
            vmem((8, 256, D), bf16),
            vmem((8, D, 256), bf16),
            vmem((8, ROWS, D), bf16),
            vmem((8, 1024, 256), f32),
            vmem((8, 1024, 256), f32),
            vmem((8, 1024, 256), bf16),
            vmem((8, 8, 256), f32),
            vmem((8, ROWS, ROWS), f32),
            vmem((8, 8, 256), f32),
            vmem((8, ROWS, ROWS), f32),
            vmem((8, 1, 256), f32),
            vmem((8, ROWS, ROWS), f32),
            vmem((2, 1024, 256), f32),
            vmem((8, 256), f32),
            vmem((8, 256), f32),
            vmem((16, 8, 256), f32),
            vmem((8, 8, ROWS), f32),
            vmem((16, 16, ROWS), f32),
            vmem((8, 16, ROWS), f32),
            vmem((8, 256, D), bf16),
            vmem((8, ROWS, D), bf16),
            vmem((8, ROWS, D), bf16),
            vmem((LAND, D), bf16),
            vmem((LAND, D), bf16),
            smem((16,), jnp.int32),
            vmem((2, ROWS, D), bf16),
            vmem((2, ROWS, D), f32),
            vmem((16, ROWS), f32),
            pltpu.SemaphoreType.DMA((8,)),
            pltpu.SemaphoreType.DMA((N_MSG,)),
            pltpu.SemaphoreType.DMA((N_MSG,)),
        ],
        compiler_params=pltpu.CompilerParams(
            collective_id=0, has_side_effects=True, vmem_limit_bytes=60 * 1024 * 1024
        ),
        name="contrast",
    )(log_scale, pairing, image_embed, text_embed)
    return pl.pallas_call(
        epilogue,
        out_shape=[grad, grad, scalar, scalar],
        in_specs=[in_vmem] * 5,
        out_specs=[in_vmem] * 2 + [in_smem] * 2,
        compiler_params=pltpu.CompilerParams(vmem_limit_bytes=60 * 1024 * 1024),
        name="back_norm",
    )(sums, image_embed, text_embed, unit_img, unit_txt)


def solution(mesh):
    return jax.shard_map(
        local,
        mesh=mesh,
        in_specs=(P(("blk", "grp"), None), P(("blk", "grp"), None), P(), P()),
        out_specs=(P(("blk", "grp"), None), P(("blk", "grp"), None), P(), P()),
        check_vma=False,
    )
```

```python
import jax
import jax.numpy as jnp
from jax import lax
from jax.experimental import pallas as pl
from jax.experimental.pallas import tpu as pltpu
from jax.sharding import PartitionSpec as P

f32, bf16 = jnp.float32, jnp.bfloat16
MESH = pl.DeviceIdType.MESH
CAP = 30.0
ROWS, D, BATCH = 128, 1280, 16384
ARRIVAL = ((0, 0), (1, 0), (3, 0), (0, 1), (2, 0), (1, 1), (3, 1), (2, 1))
REDUCE = ((2, 1), (2, 0), (1, 1), (3, 1), (0, 1), (1, 0), (3, 0), (0, 0))
LAND_AT = (0, 32, 64, 128, 192, 256, 320, 384, 448, 480, 512, 544, 576, 640, 704, 768, 832)
LAND_ROWS = (32, 32, 64, 64, 64, 64, 64, 64, 32, 32, 32, 32, 64, 64, 64, 64, 64)
LAND = 896


def flip(bit, by):
    return bit + by - 2 * bit * by


def turn(place, by):
    return lax.rem(place + by, 4)


class Messages:
    def __init__(self, send, recv):
        self.send, self.recv, self.count, self.open = send, recv, 0, {}

    def take(self, count):
        first = self.count
        self.count += count
        return first

    def start(self, k, src, dst, device):
        copy = pltpu.make_async_remote_copy(
            src, dst, self.send.at[k], self.recv.at[k], device_id=device, device_id_type=MESH
        )
        copy.start()
        self.open[k] = copy

    def arrived(self, k, region, device):
        pltpu.make_async_remote_copy(
            region, region, self.send.at[k], self.recv.at[k], device_id=device, device_id_type=MESH
        ).wait_recv()

    def sent(self, *ks):
        for k in ks:
            self.open.pop(k).wait_send()

    def finish(self):
        self.sent(*list(self.open))


class Gather:
    def __init__(self, msgs, region, plus, minus, pair, me, relay=None):
        self.m, self.region, self.me, self.relay = msgs, region, me, relay
        self.plus, self.minus, self.pair = plus, minus, pair
        self.k = msgs.take(17)

    TABLE = (
        ("plus", (0, 0, 0, 64), (3, 0, 0, 64)),
        ("plus", (0, 0, 64, 64), (3, 0, 64, 64)),
        ("plus", (3, 0, 0, 64), (2, 0, 0, 64)),
        ("plus", (0, 1, 0, 32), (3, 1, 0, 32)),
        ("plus", (3, 1, 0, 32), (2, 1, 0, 32)),
        ("minus", (0, 0, 64, 64), (1, 0, 64, 64)),
        ("minus", (0, 0, 0, 64), (1, 0, 0, 64)),
        ("minus", (1, 0, 64, 64), (2, 0, 64, 64)),
        ("minus", (0, 1, 32, 32), (1, 1, 32, 32)),
        ("minus", (1, 1, 32, 32), (2, 1, 32, 32)),
        ("pair", (0, 0, 0, 64), (0, 1, 0, 64)),
        ("pair", (0, 0, 64, 64), (0, 1, 64, 64)),
        ("pair", (1, 0, 64, 64), (1, 1, 64, 64)),
        ("pair", (3, 0, 64, 64), (3, 1, 64, 64)),
        ("pair", (2, 0, 64, 64), (2, 1, 64, 64)),
        ("plus", (0, 1, 32, 32), (3, 1, 32, 32)),
        ("minus", (0, 1, 0, 32), (1, 1, 0, 32)),
    )

    def go(self, *ks):
        for k in ks:
            way, here, _ = self.TABLE[k]
            ref = self.region(*here)
            self.m.start(self.k + k, ref, ref, getattr(self, way))

    def sent(self, *ks):
        self.m.sent(*(self.k + k for k in ks))

    def got(self, *ks):
        for k in ks:
            self.m.arrived(self.k + k, self.region(*self.TABLE[k][2]), self.me)
            if self.relay is not None:
                self.relay(k, self.TABLE[k][2])


class Reduce:
    TABLE = (
        ("plus", (2, 1), 0, 32),
        ("minus", (2, 1), 32, 32),
        ("pair", (2, 1), 64, 64),
        ("pair", (1, 1), 64, 64),
        ("plus", (1, 1), 0, 64),
        ("pair", (3, 1), 64, 64),
        ("minus", (3, 1), 0, 64),
        ("pair", (0, 1), 64, 64),
        ("plus", (2, 0), 0, 32),
        ("minus", (2, 0), 32, 32),
        ("plus", (2, 0), 64, 32),
        ("minus", (2, 0), 96, 32),
        ("pair", (0, 1), 0, 64),
        ("plus", (1, 0), 0, 64),
        ("plus", (1, 0), 64, 64),
        ("minus", (3, 0), 0, 64),
        ("minus", (3, 0), 64, 64),
    )

    def __init__(self, msgs, part, land, plus, minus, pair, me):
        self.m, self.part, self.land, self.me = msgs, part, land, me
        self.plus, self.minus, self.pair = plus, minus, pair
        self.k = msgs.take(17)

    def where(self, k):
        return self.land.at[pl.ds(LAND_AT[k], LAND_ROWS[k])]

    def go(self, *ks):
        for k in ks:
            way, place, low, rows = self.TABLE[k]
            self.m.start(self.k + k, self.part(place, low, rows), self.where(k), getattr(self, way))

    def sent(self, *ks):
        self.m.sent(*(self.k + k for k in ks))

    def got(self, *ks):
        for k in ks:
            self.m.arrived(self.k + k, self.where(k), self.me)

    def add(self, place, low, rows, *landed):
        ref = self.part(place, low, rows)
        total = ref[...].astype(f32)
        for at in landed:
            total = total + self.land[pl.ds(at, rows)].astype(f32)
        ref[...] = total.astype(bf16)

    def step(self, i):
        if i == 0:
            self.go(0, 1, 2)
        if i == 1:
            self.go(8, 9)
        if i == 2:
            self.go(3)
            self.got(0)
            self.add((1, 1), 0, 32, LAND_AT[0])
            self.go(4)
        if i == 3:
            self.go(5)
            self.got(1)
            self.add((3, 1), 32, 32, LAND_AT[1])
            self.go(6)
        if i == 4:
            self.go(7)
            self.got(2)
            self.add((2, 0), 64, 64, LAND_AT[2])
            self.go(10, 11)
        if i == 5:
            self.got(8)
            self.add((1, 0), 0, 32, LAND_AT[8])
            self.go(13)
        if i == 6:
            self.got(9)
            self.add((3, 0), 32, 32, LAND_AT[9])
            self.go(15)

    def last(self):
        self.got(4, 6)
        self.add((0, 1), 0, 64, LAND_AT[4], LAND_AT[6])
        self.go(12)
        self.got(3)
        self.add((1, 0), 64, 64, LAND_AT[3])
        self.got(10)
        self.add((1, 0), 64, 32, LAND_AT[10])
        self.go(14)

    def last_ring(self):
        self.got(5)
        self.add((3, 0), 64, 64, LAND_AT[5])
        self.got(11)
        self.add((3, 0), 96, 32, LAND_AT[11])
        self.go(16)

    def total(self, low, *ks):
        self.got(*ks)
        total = self.part((0, 0), low, 64)[...].astype(f32)
        for k in ks:
            total = total + self.where(k)[...].astype(f32)
        return total


def normalize(embed):
    wide = embed.astype(f32)
    inverse = lax.rsqrt(jnp.sum(wide * wide, axis=1, keepdims=True) + 1e-06)
    return inverse, wide * inverse


def kernel(
    ls_ref, pairing_in, img_in, txt_in,
    gi_out, gt_out, sums_out,
    img, img_t, txt, cosr, hr, gr, rowacc, colacc, rowk, colk, arow, bmat, diag, slacc, posacc,
    rows_all, cols_all, sc_all, sc_mid,
    gi, gi_sib, gt, land_i, land_t,
    pairing_ref, embeds, units, sums, own_sem, send, recv,
):
    blk, grp = lax.axis_index("blk"), lax.axis_index("grp")
    x, c, y, z = grp // 2, lax.rem(grp, 2), blk // 4, lax.rem(blk, 4)
    yb = lax.rem(y, 2)
    tb = 1 - yb
    yp = y + 1 - 2 * yb
    yq = lax.rem(y + 3 + 2 * yb, 4)

    def device(x_, y_, z_, c_):
        return (y_ * 4 + z_, x_ * 2 + c_)

    me = device(x, y, z, c)
    sibling = device(x, y, z, 1 - c)
    img_peers = [
        (dx, dy, dc) for dy in (1, 0) for dx in (2, 1, 3, 0) for dc in (1, 0) if (dx, dy, dc) != (0, 0, 0)
    ]
    txt_peers = [(dz, dy) for dy in (1, 0) for dz in (2, 1, 3, 0) if (dz, dy) != (0, 0)]

    def img_peer(dx, dy, dc):
        return device(turn(x, dx), yp if dy else y, z, 1 - c if dc else c)

    def txt_peer(dz, dy):
        return device(x, yq if dy else y, turn(z, dz), c)

    own_copies = [
        pltpu.make_async_copy(src, dst, own_sem.at[i])
        for i, (src, dst) in enumerate(((img_in, embeds.at[0]), (txt_in, embeds.at[1]), (pairing_in, pairing_ref)))
    ]
    for copy in own_copies:
        copy.start()
    barrier = pltpu.get_barrier_semaphore()
    for p in img_peers:
        pl.semaphore_signal(barrier, inc=1, device_id=img_peer(*p), device_id_type=MESH)
    for p in txt_peers:
        pl.semaphore_signal(barrier, inc=1, device_id=txt_peer(*p), device_id_type=MESH)

    def pair_of(dx, dy):
        return flip(yb, dy) * 4 + turn(x, dx)

    def slot_of(dz, dy):
        return flip(tb, dy) * 4 + turn(z, dz)

    def img_region(dx, dy, low, rows, other=False):
        half = 1 - c if other else c
        return img.at[pair_of(dx, dy), pl.ds(pl.multiple_of(half * ROWS + low, 32), rows)]

    def txt_region(dz, dy, low, rows):
        return txt.at[slot_of(dz, dy), pl.ds(low, rows)]

    own_copies[0].wait()
    img_region(0, 0, 0, ROWS)[...] = normalize(embeds[0])[1].astype(bf16)
    own_copies[1].wait()
    txt_region(0, 0, 0, ROWS)[...] = normalize(embeds[1])[1].astype(bf16)

    msgs = Messages(send, recv)
    sib_k = msgs.take(18)

    def share(k, region):
        ref = img_region(*region)
        msgs.start(sib_k + k, ref, ref, sibling)

    gat_i = Gather(msgs, img_region, img_peer(1, 0, 0), img_peer(3, 0, 0), img_peer(0, 1, 0), me, share)
    gat_t = Gather(msgs, txt_region, txt_peer(1, 0), txt_peer(3, 0), txt_peer(0, 1), me)
    both = (gat_i, gat_t)

    def shared(place):
        pieces = [(k, entry[2]) for k, entry in enumerate(Gather.TABLE) if entry[2][:2] == place]
        for k, region in pieces or [(17, (0, 0, 0, ROWS))]:
            msgs.arrived(sib_k + k, img_region(*region, other=True), me)

    pl.semaphore_wait(barrier, len(img_peers) + len(txt_peers))
    for g in both:
        g.go(10, 0, 5, 11, 1, 6)
    share(17, (0, 0, 0, ROWS))

    scale = jnp.exp(jnp.full((1, 256), ls_ref[0], f32))
    factor = scale * (1.0 / CAP)
    for ref in (rowacc, colacc, rowk, colk, slacc, posacc):
        ref[...] = jnp.zeros_like(ref)

    def rows_of(slot):
        return pl.ds(pl.multiple_of(slot * ROWS, ROWS), ROWS)

    def forward(p, s):
        cos = lax.dot_general(txt[s], img_t[p], (((1,), (0,)), ((), ())), preferred_element_type=f32)
        bent = jnp.tanh(cos * factor)
        power = jnp.exp(CAP * bent)
        held = power * (1.0 - bent * bent)
        slope = held * cos
        cosr[p, rows_of(s)] = cos
        hr[p, rows_of(s)] = held
        colacc[s] += power[:, :ROWS] + power[:, ROWS:]
        colk[s] += slope[:, :ROWS] + slope[:, ROWS:]
        rowacc[p] += jnp.sum(power.reshape(16, 8, 256), axis=0)
        rowk[p] += jnp.sum(slope.reshape(16, 8, 256), axis=0)

    def pair_at(i):
        dx = jnp.where((i == 1) | (i == 5), 1, 0) + jnp.where((i == 2) | (i == 6), 3, 0)
        dx = dx + jnp.where((i == 4) | (i == 7), 2, 0)
        dy = jnp.where((i == 3) | (i >= 5), 1, 0)
        return flip(yb, dy) * 4 + turn(x, dx)

    slots = [slot_of(*place) for place in ARRIVAL]

    def batch(first, last, members, unroll=1):
        def body(i, carry):
            for j in members:
                forward(pair_at(i), slots[j])
            return carry

        lax.fori_loop(first, last, body, 0, unroll=unroll)

    def turned(place):
        shared(place)
        p = pair_of(*place)
        img_t[p] = img[p].T

    turned((0, 0))
    batch(0, 1, (0,))
    for g in both:
        g.got(0, 5, 10)
        g.go(2, 7, 12, 3, 8, 15, 16)
    for g in both:
        g.got(1)
        g.go(13)
        g.got(6, 11)
    batch(0, 1, (1, 2, 3))
    turned((1, 0))
    batch(1, 2, (0, 1, 2, 3))
    turned((3, 0))
    batch(2, 3, (0, 1, 2, 3))
    for g in both:
        g.got(7)
        g.go(14)
        g.got(2, 12)
    turned((0, 1))
    batch(3, 4, (0, 1, 2, 3))
    batch(0, 4, (4,), unroll=4)
    turned((2, 0))
    for g in both:
        g.got(3)
        g.go(4)
        g.got(8)
        g.go(9)
    batch(4, 5, (0, 1, 2, 3, 4))
    for g in both:
        g.got(13, 15, 16)
    batch(0, 5, (5, 6), unroll=5)
    turned((1, 1))
    batch(5, 6, (0, 1, 2, 3, 4, 5, 6))
    gat_i.got(4, 9)
    turned((3, 1))
    batch(6, 7, (0, 1, 2, 3, 4, 5, 6))
    gat_i.got(14)
    gat_t.got(4, 9, 14)
    batch(0, 7, (7,), unroll=7)
    turned((2, 1))
    batch(7, 8, (0, 1, 2, 3, 4, 5, 6, 7))

    img_me = yb * 8 + x * 2 + c
    txt_me = tb * 4 + z

    def img_index(dx, dy, dc):
        return flip(yb, dy) * 8 + turn(x, dx) * 2 + flip(c, dc)

    rows_all[img_me] = jnp.concatenate([jnp.sum(rowacc[p], axis=0, keepdims=True) for p in range(8)], axis=0)
    cols_all[txt_me] = jnp.concatenate(
        [jnp.sum(colacc[s].T, axis=0, keepdims=True) for s in range(8)], axis=0
    )
    k_rows, k_cols = msgs.take(len(img_peers)), msgs.take(len(txt_peers))
    for far in (1, 0):
        for i, p in enumerate(txt_peers):
            if p[1] == far:
                msgs.start(k_cols + i, cols_all.at[txt_me], cols_all.at[txt_me], txt_peer(*p))
        for i, p in enumerate(img_peers):
            if p[1] == far:
                msgs.start(k_rows + i, rows_all.at[img_me], rows_all.at[img_me], img_peer(*p))

    def collect_img(first, ref):
        for i, (dx, dy, dc) in enumerate(img_peers):
            msgs.arrived(first + i, ref.at[img_index((4 - dx) % 4, dy, dc)], me)

    def collect_txt(first, ref):
        for i, (dz, dy) in enumerate(txt_peers):
            msgs.arrived(first + i, ref.at[slot_of((4 - dz) % 4, dy)], me)

    def add_up(ref, first, last):
        total = ref[first]
        for i in range(first + 1, last):
            total = total + ref[i]
        return total

    own_copies[2].wait()
    lane = lax.broadcasted_iota(jnp.int32, (ROWS, 256), 1)
    diagonal = lane == lax.broadcasted_iota(jnp.int32, (ROWS, 256), 0) + c * ROWS
    pair_mine = (pair_of(0, 0), pair_of(0, 1))

    def matching(s, carry):
        slot_blk = jnp.where(s // 4 == tb, y, yq) * 4 + lax.rem(s, 4)
        for dy in range(2):
            partner_of = pairing_ref[(yp if dy else y) * 4 + z]
            match = jnp.where(partner_of == slot_blk, 1.0, 0.0).astype(f32)
            partner = jnp.where(diagonal, match, 0.0)
            cos = cosr[pair_mine[dy], rows_of(s)]
            bent = jnp.tanh(cos * factor)
            taken = scale * (partner * (1.0 - bent * bent))
            diag[dy, rows_of(s)] = taken
            posacc[...] += jnp.sum((CAP * bent * partner).reshape(16, 8, 256), axis=0)
            slacc[...] += jnp.sum((taken * cos).reshape(16, 8, 256), axis=0)
        return carry

    lax.fori_loop(0, 8, matching, 0, unroll=2)
    row_slope = jnp.concatenate([jnp.sum(rowk[p], axis=0, keepdims=True) for p in range(8)], axis=0)
    col_slope = jnp.concatenate([jnp.sum(colk[s].T, axis=0, keepdims=True) for s in range(8)], axis=0)
    for g in both:
        g.sent(*range(17))
    msgs.sent(*range(sib_k, sib_k + 18))

    collect_txt(k_cols, cols_all)
    col_sum = add_up(cols_all, 0, 8)
    col_weight = (0.5 * scale[:, :ROWS]) / col_sum
    for s in range(8):
        bmat[s] = jnp.broadcast_to(col_weight[s : s + 1], (ROWS, ROWS)).T
    collect_img(k_rows, rows_all)
    row_sum = add_up(rows_all, 0, 16)
    row_weight = (0.5 * scale) / row_sum
    for p in range(8):
        arow[p] = row_weight[p : p + 1]

    def tile(p, s, matched=None):
        b = bmat[s]
        g = hr[p, rows_of(s)] * (arow[p] + jnp.concatenate([b, b], axis=1))
        if matched is not None:
            g = g - diag[matched, rows_of(s)]
        gr[p, rows_of(s)] = g.astype(bf16)

    def gradient(place, first=1):
        p = pair_of(*place)

        def body(i, carry):
            tile(p, lax.rem(slot_of(2, 1) + i, 8), place[1] if place[0] == 0 else None)
            return carry

        lax.fori_loop(first, 8, body, 0, unroll=4 if first == 0 else 7)

    def send_sums():
        sub = lax.broadcasted_iota(jnp.int32, (8, 256), 0)
        half = lax.broadcasted_iota(jnp.int32, (8, 256), 1) // ROWS
        row_part = jnp.where((sub == pair_mine[0]) & (half == c), jnp.log(row_sum), 0.0) - 2.0 * posacc[...]
        col_part = jnp.where(sub[:, :ROWS] == txt_me, jnp.log(col_sum), 0.0)
        slope = row_weight * row_slope - slacc[...]
        sc_all[img_me, pl.ds(0, 8)] = row_part[:, :ROWS] + row_part[:, ROWS:] + col_part
        sc_all[img_me, pl.ds(8, 8)] = slope[:, :ROWS] + slope[:, ROWS:] + col_weight * col_slope
        for i, p in enumerate(img_peers):
            msgs.start(k_sc + i, sc_all.at[img_me], sc_all.at[img_me], img_peer(*p))

    k_sc = msgs.take(len(img_peers))

    k_sib = msgs.take(8)
    own = pl.ds(pl.multiple_of(c * ROWS, ROWS), ROWS)
    others = pl.ds(pl.multiple_of((1 - c) * ROWS, ROWS), ROWS)

    def img_part(place, low, rows):
        return gi.at[REDUCE.index(place), pl.ds(pl.multiple_of(c * ROWS + low, 32), rows)]

    def txt_part(place, low, rows):
        return gt.at[REDUCE.index(place), pl.ds(low, rows)]

    red_i = Reduce(msgs, img_part, land_i, img_peer(1, 0, 0), img_peer(3, 0, 0), img_peer(0, 1, 0), me)
    red_t = Reduce(msgs, txt_part, land_t, txt_peer(1, 0), txt_peer(3, 0), txt_peer(0, 1), me)
    k_mid = msgs.take(len(txt_peers))

    def img_product(i):
        gi[i] = lax.dot_general(
            gr[pair_of(*REDUCE[i])], txt[...].reshape(8 * ROWS, D), (((0,), (0,)), ((), ())), preferred_element_type=f32
        ).astype(bf16)
        msgs.start(k_sib + i, gi.at[i, others], gi_sib.at[i], sibling)

    def img_send(i):
        msgs.arrived(k_sib + i, gi_sib.at[i], me)
        gi[i, own] = (gi[i, own].astype(f32) + gi_sib[i].astype(f32)).astype(bf16)
        red_i.step(i)

    def txt_product(i):
        s = slot_of(*REDUCE[i])
        lhs = jnp.concatenate([gr[q, rows_of(s)] for q in range(8)], axis=1)
        gt[i] = lax.dot_general(
            lhs, img[...].reshape(16 * ROWS, D), (((1,), (0,)), ((), ())), preferred_element_type=f32
        ).astype(bf16)
        red_t.step(i)

    gradient(REDUCE[0], 0)
    img_product(0)
    for place in REDUCE[1:]:
        tile(pair_of(*place), slot_of(2, 1), place[1] if place[0] == 0 else None)
    txt_product(0)
    for place in REDUCE[1:]:
        gradient(place)
    img_send(0)
    for i in range(1, 8):
        img_product(i)
        if i > 1:
            img_send(i - 1)
        txt_product(i)
        if i == 1:
            send_sums()
        if i == 4:
            collect_img(k_sc, sc_all)
            sc_mid[txt_me] = add_up(sc_all, 0, 16)
            for j, peer in enumerate(txt_peers):
                msgs.start(k_mid + j, sc_mid.at[txt_me], sc_mid.at[txt_me], txt_peer(*peer))
    img_send(7)
    for r in (red_i, red_t):
        r.last()
    for r in (red_i, red_t):
        r.last_ring()
    collect_txt(k_mid, sc_mid)
    sums[...] = add_up(sc_mid, 0, 4) + add_up(sc_mid, 4, 8)
    out_copies = [pltpu.make_async_copy(sums, sums_out, own_sem.at[3])]
    out_copies[0].start()
    for first, count in ((k_rows, 15), (k_cols, 7), (k_sc, 15), (k_mid, 7), (k_sib, 8)):
        msgs.sent(*range(first, first + count))
    for r in (red_i, red_t):
        r.sent(*range(12))
    for low, ks in ((64, (7, 14, 16)), (0, (13, 15, 12))):
        for n, (r, out) in enumerate(((red_i, gi_out), (red_t, gt_out))):
            part = pl.ds(low, 64)
            units[n, part] = r.total(low, *ks).astype(bf16)
            copy = pltpu.make_async_copy(units.at[n, part], out.at[part], own_sem.at[3 + len(out_copies)])
            copy.start()
            out_copies.append(copy)
    msgs.finish()
    for copy in out_copies:
        copy.wait()


def epilogue(sums, img_in, txt_in, gi_in, gt_in, gi_out, gt_out, loss_out, gls_out):
    for embed, grad, out in ((img_in, gi_in, gi_out), (txt_in, gt_in, gt_out)):
        inverse, unit = normalize(embed[...])
        grad_unit = grad[...].astype(f32)
        inner = jnp.sum(unit * grad_unit, axis=1, keepdims=True)
        out[...] = inverse * (grad_unit - unit * inner)
    loss_out[0] = jnp.sum(sums[:8]) * (1.0 / (2.0 * BATCH))
    gls_out[0] = jnp.sum(sums[8:]) * (1.0 / BATCH)


N_MSG = 17 + 17 + 18 + 15 + 7 + 15 + 8 + 17 + 17 + 7


def local(image_embed, text_embed, log_scale, pairing):
    vmem, smem = pltpu.VMEM, pltpu.SMEM
    in_hbm, in_vmem, in_smem = (pl.BlockSpec(memory_space=m) for m in (pltpu.HBM, vmem, smem))
    grad, unit = jax.ShapeDtypeStruct((ROWS, D), f32), jax.ShapeDtypeStruct((ROWS, D), bf16)
    scalar = jax.ShapeDtypeStruct((1,), f32)
    unit_img, unit_txt, sums = pl.pallas_call(
        kernel,
        out_shape=[unit, unit, jax.ShapeDtypeStruct((16, ROWS), f32)],
        in_specs=[in_smem] + [in_hbm] * 3,
        out_specs=[in_hbm] * 3,
        scratch_shapes=[
            vmem((8, 256, D), bf16),
            vmem((8, D, 256), bf16),
            vmem((8, ROWS, D), bf16),
            vmem((8, 1024, 256), f32),
            vmem((8, 1024, 256), f32),
            vmem((8, 1024, 256), bf16),
            vmem((8, 8, 256), f32),
            vmem((8, ROWS, ROWS), f32),
            vmem((8, 8, 256), f32),
            vmem((8, ROWS, ROWS), f32),
            vmem((8, 1, 256), f32),
            vmem((8, ROWS, ROWS), f32),
            vmem((2, 1024, 256), f32),
            vmem((8, 256), f32),
            vmem((8, 256), f32),
            vmem((16, 8, 256), f32),
            vmem((8, 8, ROWS), f32),
            vmem((16, 16, ROWS), f32),
            vmem((8, 16, ROWS), f32),
            vmem((8, 256, D), bf16),
            vmem((8, ROWS, D), bf16),
            vmem((8, ROWS, D), bf16),
            vmem((LAND, D), bf16),
            vmem((LAND, D), bf16),
            smem((16,), jnp.int32),
            vmem((2, ROWS, D), bf16),
            vmem((2, ROWS, D), bf16),
            vmem((16, ROWS), f32),
            pltpu.SemaphoreType.DMA((8,)),
            pltpu.SemaphoreType.DMA((N_MSG,)),
            pltpu.SemaphoreType.DMA((N_MSG,)),
        ],
        compiler_params=pltpu.CompilerParams(
            collective_id=0, has_side_effects=True, vmem_limit_bytes=60 * 1024 * 1024
        ),
        name="contrast",
    )(log_scale, pairing, image_embed, text_embed)
    return pl.pallas_call(
        epilogue,
        out_shape=[grad, grad, scalar, scalar],
        in_specs=[in_vmem] * 5,
        out_specs=[in_vmem] * 2 + [in_smem] * 2,
        compiler_params=pltpu.CompilerParams(vmem_limit_bytes=60 * 1024 * 1024),
        name="back_norm",
    )(sums, image_embed, text_embed, unit_img, unit_txt)


def solution(mesh):
    return jax.shard_map(
        local,
        mesh=mesh,
        in_specs=(P(("blk", "grp"), None), P(("blk", "grp"), None), P(), P()),
        out_specs=(P(("blk", "grp"), None), P(("blk", "grp"), None), P(), P()),
        check_vma=False,
    )
```
